512 devices in a mesh: ctx: 32 (over z, core), dp: 16 (over x, y).
Axes of the slice: x: 4, y: 4, z: 16, core: 2. Of those that a mesh axis runs over, the one named last changes fastest.
Arguments:
- queries: bfloat16 [65536, 3072], P(('dp', 'ctx')), parts along dimension 0, may hold values from -96 to 96
- key_vectors: bfloat16 [65536, 512], P(('dp', 'ctx')), parts along dimension 0, may hold values from -4 to 4
- value_matrix: bfloat16 [65536, 512], P(('dp', 'ctx')), parts along dimension 0, may hold values from -6 to 6
- out_grad: bfloat16 [65536, 3072], P(('dp', 'ctx')), parts along dimension 0, may hold values from -6 to 6
- clip_lengths: int32 [336], P('dp'), parts along dimension 0, may hold values from 1 to 6, 64 in all
- clip_full: int32 [336], P('dp'), parts along dimension 0, may hold values 0 or 1
Outputs:
- attended: bfloat16 [65536, 3072], P(('dp', 'ctx')), parts along dimension 0
- query_grad: bfloat16 [65536, 3072], P(('dp', 'ctx')), parts along dimension 0
- gradient_of_keys: bfloat16 [65536, 512], P(('dp', 'ctx')), parts along dimension 0
- gradient_of_values: bfloat16 [65536, 512], P(('dp', 'ctx')), parts along dimension 0
The draws below stay inside these ranges and needn't reach their ends.
There are 16 independent parts, one for each index of `dp`. The reference program is written for one: setup_inputs(seed, part) draws one part's arguments, and reference() takes and returns one part's arrays. A program takes and returns all parts, laid end to end along the dimension named above; each array names one. Nothing has to cross between parts.
Inputs may be any that keep to these rules, and one draw needn't show every extreme that they name: `clip_lengths`: clip lengths in mask blocks of 64 tokens; they sum to 64 and the largest is 6.
All inputs are finite; a program needn't handle non-finite values.
Results may differ from the reference program's by a relative error of at most 0.01.
Values may be sent and summed in bfloat16 or wider, within the bound.
A program may use at most 64 MiB of HBM per device.

```python
import math
import jax
import jax.numpy as jnp
import numpy as np
from jax import lax

QUERY_HEADS = 24
KEY_VALUE_HEADS = 4
HEAD_WIDTH = 128
TOK_DEV = 128
BLOCK = 64
GROUP = 6
PACKED_TOKENS = 4096
NBLOCKS = 64
CLIP_BLOCKS = 6
CLIPS = 21
N_CTX = 32


def shared_keys(key):
    return jax.random.truncated_normal(key, -4.0, 4.0, (PACKED_TOKENS, KEY_VALUE_HEADS * HEAD_WIDTH), jnp.float32)


def draw_key_vectors(key, part):
    starting_keys = shared_keys(key)
    return starting_keys.astype(jnp.bfloat16)


def draw_queries(key, part):
    key = jax.random.fold_in(key, 5)
    noise = jax.random.truncated_normal(key, -4.0, 4.0, (PACKED_TOKENS, QUERY_HEADS * HEAD_WIDTH), jnp.float32)
    return noise.astype(jnp.bfloat16)


def set_ends(array, key, smallest, largest):
    longest = array.shape.index(max(array.shape))
    spots = []
    for shift in (0, 1):
        where = [jax.random.randint(jax.random.fold_in(key, axis), (), 0, length) for axis, length in enumerate(array.shape)]
        where[longest] = (where[longest] + shift) % array.shape[longest]
        spots.append(tuple(where))
    return array.at[spots[0]].set(smallest).at[spots[1]].set(largest)


def block_levels(key, shape, split, low, top_value):
    loudness = 1.0
    for axis_at, blocks in split:
        steps = jax.random.uniform(jax.random.fold_in(jax.random.fold_in(key, 6), axis_at), (blocks,), jnp.float32, low / len(split), top_value / len(split))
        loudness = loudness * jnp.repeat(jnp.exp(steps), shape[axis_at] // blocks).reshape((-1,) + (1,) * (len(shape) - 1 - axis_at))
    return loudness


def profile(number_of, total, bound, slope):
    loads = [(1 << 20) // math.isqrt(standing ** slope) + 1 for standing in range(2, number_of + 1)]
    spare, counts = total - bound - (number_of - 1), [1] * (number_of - 1)
    while spare > 0:
        candidates = [i for i in range(number_of - 1) if counts[i] < bound]
        whole, budget = sum([loads[i] for i in candidates]), spare
        for i in candidates:
            more = min(bound - counts[i], max(1, budget * loads[i] // whole), spare)
            counts[i] = counts[i] + more
            spare = spare - more
    return np.array([bound] + counts)


def ragged(stream_key, amount, total, most, lean):
    if amount == 2:
        one = jax.random.randint(stream_key, (), max(1, total - most), min(most, total - 1) + 1)
        return jnp.stack([one, total - one])
    lengths = jnp.asarray(profile(amount, total, most, lean), jnp.int32)
    twos = (amount - 1) // 2
    source_of, taker = lengths[1:1 + 2 * twos:2], lengths[2:2 + 2 * twos:2]
    room = jnp.minimum(source_of - 1, most - taker)
    shifted = jax.random.randint(jax.random.fold_in(stream_key, 1), (twos,), 0, 1 << 20) % (room + 1)
    lengths = lengths.at[1:1 + 2 * twos:2].set(source_of - shifted).at[2:2 + 2 * twos:2].set(taker + shifted)
    return lengths[jax.random.permutation(jax.random.fold_in(stream_key, 2), amount)]


def normal_values(rng, extent, width, most, split=(), held_as=jnp.bfloat16):
    values = width * jax.random.normal(rng, extent, jnp.float32)
    if split:
        values = values * block_levels(rng, extent, split, -0.22, 0.18)
    return jnp.clip(values, -most, most).astype(held_as)


def setup_inputs(seed: int = 0, part: int = 0) -> dict:
    keys = jax.random.split(jax.random.key(seed), 7)
    own_keys = jax.random.split(jax.random.fold_in(keys[6], part), 7)
    return {
        "queries": draw_queries(jax.random.fold_in(jax.random.fold_in(keys[6], part), 71), part),
        "key_vectors": draw_key_vectors(jax.random.fold_in(jax.random.fold_in(keys[6], part), 71), part),
        "value_matrix": normal_values(own_keys[2], (PACKED_TOKENS, KEY_VALUE_HEADS * HEAD_WIDTH), 1.0, 6.0, ((0, 32),)),
        "out_grad": normal_values(own_keys[3], (PACKED_TOKENS, QUERY_HEADS * HEAD_WIDTH), 1.0, 6.0, ((0, 32),)),
        "clip_lengths": ragged(own_keys[4], CLIPS, NBLOCKS, CLIP_BLOCKS, 1).astype(jnp.int32),
        "clip_full": set_ends((jax.random.randint(own_keys[5], (CLIPS,), 0, 2) < 1).astype(jnp.int32), jax.random.fold_in(own_keys[5], 1), 0, 1),
    }


def clip_index(blocks, clip_ends):
    return jnp.sum((blocks[:, None] >= clip_ends[None, :]).astype(jnp.int32), axis=1, dtype=jnp.int32)


def reference(queries, key_vectors, value_matrix, out_grad, clip_lengths, clip_full):
    score_scale = HEAD_WIDTH ** -0.5
    positions = jnp.arange(PACKED_TOKENS, dtype=jnp.int32)
    blocks = positions // BLOCK
    clip_ends = jnp.cumsum(clip_lengths, dtype=jnp.int32)
    token_clip = clip_index(blocks, clip_ends)
    token_full = clip_full[token_clip] > 0
    allowed = (token_clip[:, None] == token_clip[None, :]) & (token_full[:, None] | (blocks[None, :] <= blocks[:, None]))

    def single_group(group_index):
        key_head = lax.dynamic_slice_in_dim(key_vectors, group_index * HEAD_WIDTH, HEAD_WIDTH, 1)
        value_head = lax.dynamic_slice_in_dim(value_matrix, group_index * HEAD_WIDTH, HEAD_WIDTH, 1)
        key_parts = jnp.zeros((N_CTX, PACKED_TOKENS, HEAD_WIDTH), jnp.float32)
        value_parts = jnp.zeros((N_CTX, PACKED_TOKENS, HEAD_WIDTH), jnp.float32)
        attn_list = []
        query_list = []
        for member in range(GROUP):
            head_index = group_index * GROUP + member
            query_head = lax.dynamic_slice_in_dim(queries, head_index * HEAD_WIDTH, HEAD_WIDTH, 1)
            grad_head = lax.dynamic_slice_in_dim(out_grad, head_index * HEAD_WIDTH, HEAD_WIDTH, 1)
            scores = jnp.dot(query_head, key_head.T, preferred_element_type=jnp.float32) * score_scale
            scores = jnp.where(allowed, scores, -jnp.inf)
            peak = jnp.max(scores, axis=1, keepdims=True)
            log_total = peak + jnp.log(jnp.sum(jnp.exp(scores - peak), axis=1, keepdims=True))
            probs = jnp.exp(scores - log_total)
            probs_low = probs.astype(jnp.bfloat16)
            attn_head = jnp.dot(probs_low, value_head, preferred_element_type=jnp.float32)
            delta = jnp.sum(grad_head.astype(jnp.float32) * attn_head, axis=1)
            dprobs = jnp.dot(grad_head, value_head.T, preferred_element_type=jnp.float32)
            dscores = (probs * (dprobs - delta[:, None])).astype(jnp.bfloat16)
            query_list.append((score_scale * jnp.dot(dscores, key_head, preferred_element_type=jnp.float32)).astype(jnp.bfloat16))
            attn_list.append(attn_head.astype(jnp.bfloat16))
            split_scores = dscores.astype(jnp.float32).reshape(N_CTX, TOK_DEV, PACKED_TOKENS)
            split_probs = probs_low.astype(jnp.float32).reshape(N_CTX, TOK_DEV, PACKED_TOKENS)
            split_queries = query_head.astype(jnp.float32).reshape(N_CTX, TOK_DEV, HEAD_WIDTH)
            split_grads = grad_head.astype(jnp.float32).reshape(N_CTX, TOK_DEV, HEAD_WIDTH)
            key_parts = key_parts + score_scale * jnp.einsum("nqk,nqd->nkd", split_scores, split_queries)
            value_parts = value_parts + jnp.einsum("nqk,nqd->nkd", split_probs, split_grads)
        key_low = lax.optimization_barrier(key_parts.astype(jnp.bfloat16))
        value_low = lax.optimization_barrier(value_parts.astype(jnp.bfloat16))
        key_sum = jnp.sum(key_low.astype(jnp.float32), axis=0).astype(jnp.bfloat16)
        value_sum = jnp.sum(value_low.astype(jnp.float32), axis=0).astype(jnp.bfloat16)
        return jnp.stack(attn_list), jnp.stack(query_list), key_sum, value_sum

    collected_results = lax.map(single_group, jnp.arange(KEY_VALUE_HEADS, dtype=jnp.int32))
    attended = collected_results[0].transpose(2, 0, 1, 3).reshape(PACKED_TOKENS, QUERY_HEADS * HEAD_WIDTH)
    query_grad = collected_results[1].transpose(2, 0, 1, 3).reshape(PACKED_TOKENS, QUERY_HEADS * HEAD_WIDTH)
    gradient_of_keys = collected_results[2].transpose(1, 0, 2).reshape(PACKED_TOKENS, KEY_VALUE_HEADS * HEAD_WIDTH)
    gradient_of_values = collected_results[3].transpose(1, 0, 2).reshape(PACKED_TOKENS, KEY_VALUE_HEADS * HEAD_WIDTH)
    return attended, query_grad, gradient_of_keys, gradient_of_values
```

```python
import jax
import jax.numpy as jnp
from jax import lax
from jax.experimental import pallas as pl
from jax.experimental.pallas import tpu as pltpu
from jax.sharding import PartitionSpec as P

MESH = pl.DeviceIdType.MESH
WIDTH = 128
BLOCK = 64
REACH = 6
CHIP_BLOCKS = 4
WINDOW = CHIP_BLOCKS + 2 * (REACH - 1)
OWN = REACH - 1
LEFT = OWN - CHIP_BLOCKS
RIGHT = OWN + CHIP_BLOCKS
HEADS = 2
SPAN = REACH * BLOCK
LOG2E = 1.4426950408889634


def kernel(
    q_hbm, k_hbm, v_hbm, g_hbm, lengths, fulls,
    o_hbm, dq_hbm, dk_out, dv_out,
    q0, q1, g0, g1, k0, k1, v0, v1, o0, o1, dq0, dq1,
    parts, s0, s1, edge, x0, x1, r0, r1, p0, p1, first, seen,
    kv_send, kv_recv, kv_own, q_own, q_send, q_recv, f_send, f_recv,
    x_send, x_recv, r_send, r_recv, p_send, p_recv, o_own, o_send, o_recv,
):
    q, g, k, v, o, dq = (q0, q1), (g0, g1), (k0, k1), (v0, v1), (o0, o1), (dq0, dq1)
    s, x, r, p = (s0, s1), (x0, x1), (r0, r1), (p0, p1)
    rows = 2 * BLOCK
    group = q0.shape[1] // WIDTH
    cols = group * WIDTH
    me = lax.axis_index("ctx")
    chips = lax.axis_size("ctx") // 2
    chip, core = me // 2, lax.rem(me, 2)
    other = 1 - core
    after = lax.rem(chip + 1, chips)
    before = lax.rem(chip + chips - 1, chips)
    peer = 2 * chip + other

    def away(src, dst, send, recv, target):
        pltpu.make_async_remote_copy(
            src_ref=src, dst_ref=dst, send_sem=send, recv_sem=recv,
            device_id={"ctx": target}, device_id_type=MESH,
        ).start()

    def wait(ref, sem):
        pltpu.make_async_copy(ref, ref, sem).wait()

    def head_columns(head, width):
        return pl.ds(pl.multiple_of(head * width, WIDTH), width)

    barrier = pltpu.get_barrier_semaphore()
    for device in (peer, 2 * before, 2 * before + 1, 2 * after, 2 * after + 1):
        pl.semaphore_signal(barrier, inc=1, device_id={"ctx": device}, device_id_type=MESH)
    pl.semaphore_wait(barrier, 5)

    own_blocks = pl.ds(OWN + 2 * core, 2)
    in_after = pl.ds(LEFT + 2 * core, 2)
    in_before = pl.ds(RIGHT + 2 * core, 2)
    token_rows = pl.ds(pl.multiple_of(core * rows, rows), rows)
    peer_rows = pl.ds(pl.multiple_of(other * rows, rows), rows)

    def send_inputs(h):
        for target in (0, 1):
            head = head_columns(HEADS * target + h, WIDTH)
            for src, dst in ((k_hbm, k[h]), (v_hbm, v[h])):
                away(src.at[:, :, head], dst.at[in_after], kv_send.at[h],
                     kv_recv.at[h, core], 2 * after + target)
                away(src.at[:, :, head], dst.at[in_before], kv_send.at[h],
                     kv_recv.at[h, 2 + core], 2 * before + target)
        mine, theirs = HEADS * core + h, HEADS * other + h
        for src, dst in ((q_hbm, q[h]), (g_hbm, g[h])):
            away(src.at[:, head_columns(theirs, cols)], dst.at[token_rows], q_send.at[h],
                 q_recv.at[h], peer)
        for src, dst in ((k_hbm, k[h]), (v_hbm, v[h])):
            away(src.at[:, :, head_columns(theirs, WIDTH)], dst.at[own_blocks], kv_send.at[h],
                 kv_recv.at[h, 4], peer)
            pltpu.make_async_copy(
                src.at[:, :, head_columns(mine, WIDTH)], dst.at[own_blocks], kv_own.at[h]
            ).start()
        for src, dst in ((q_hbm, q[h]), (g_hbm, g[h])):
            pltpu.make_async_copy(
                src.at[:, head_columns(mine, cols)], dst.at[token_rows], q_own.at[h]
            ).start()

    def forward(h):
        wait(k[h].at[:4], kv_recv.at[h, 1])
        for ref in (k[h], v[h]):
            away(ref.at[OWN - 1], ref.at[0], f_send.at[h], f_recv.at[h, 0], 2 * after + core)
        wait(k[h].at[:4], kv_recv.at[h, 2])
        for ref in (k[h], v[h]):
            away(ref.at[RIGHT], ref.at[WINDOW - 1], f_send.at[h], f_recv.at[h, 1], 2 * before + core)

    def wait_inputs(h):
        wait(q[h], q_own.at[h])
        wait(q[h], q_recv.at[h])
        wait(k[h].at[:4], kv_own.at[h])
        for slot in (0, 3, 4):
            wait(k[h].at[:4], kv_recv.at[h, slot])
        for side in (0, 1):
            wait(k[h].at[:2], f_recv.at[h, side])

    score_scale = WIDTH**-0.5

    def tile(h, t):
        tokens = pl.ds(pl.multiple_of(t * BLOCK, BLOCK), BLOCK)
        begin = first[t]
        count = seen[t]

        def windowed(ref):
            return jnp.concatenate([ref[begin + b] for b in range(REACH)], axis=0)

        keys, values = windowed(k[h]), windowed(v[h])

        def stacked(ref):
            return jnp.concatenate(
                [ref[tokens, pl.ds(m * WIDTH, WIDTH)] for m in range(group)], axis=0
            )

        query, grad = stacked(q[h]), stacked(g[h])
        across = (((1,), (1,)), ((), ()))
        scores = lax.dot_general(keys, query, across, preferred_element_type=jnp.float32)
        logits = [scores[:BLOCK] * (score_scale * LOG2E)]
        for b in range(1, REACH):
            bias = jnp.where(b < count, 0.0, -jnp.inf).astype(jnp.float32)
            logits.append(scores[b * BLOCK : (b + 1) * BLOCK] * (score_scale * LOG2E) + bias)
        logits = jnp.concatenate(logits, axis=0)
        peak = jnp.max(logits, axis=0, keepdims=True)
        weight = jnp.exp2(logits - peak)
        probs = weight * (1.0 / jnp.sum(weight, axis=0, keepdims=True))
        low = probs.astype(jnp.bfloat16)
        down = (((0,), (0,)), ((), ()))
        attn = lax.dot_general(values, low, down, preferred_element_type=jnp.float32)
        dprobs = lax.dot_general(values, grad, across, preferred_element_type=jnp.float32)
        delta = jnp.sum(probs * dprobs, axis=0, keepdims=True)
        dscores = (probs * (dprobs - delta)).astype(jnp.bfloat16)
        dquery = lax.dot_general(keys, dscores, down, preferred_element_type=jnp.float32)
        dkeys = jnp.dot(dscores, query, preferred_element_type=jnp.float32)
        dvalues = jnp.dot(low, grad, preferred_element_type=jnp.float32)
        for b in range(REACH):
            at = slice(b * BLOCK, (b + 1) * BLOCK)
            parts[t, b + 1, :, :WIDTH] = dkeys[at]
            parts[t, b + 1, :, WIDTH:] = dvalues[at]
        attn = attn.astype(jnp.bfloat16).T
        dquery = (dquery * score_scale).astype(jnp.bfloat16).T
        for m in range(group):
            at = pl.ds(m * WIDTH, WIDTH)
            o[h][tokens, at] = attn[m * BLOCK : (m + 1) * BLOCK]
            dq[h][tokens, at] = dquery[m * BLOCK : (m + 1) * BLOCK]

    def tiles(h, start, stop):
        def step(t, carry):
            tile(h, t)
            return carry

        lax.fori_loop(start, stop, step, 0)

    scale_row = jnp.where(
        lax.broadcasted_iota(jnp.int32, (1, 2 * WIDTH), 1) < WIDTH, score_scale, 1.0
    ).astype(jnp.float32)

    def window_sum(w):
        total = None
        for t in range(max(0, w - 2 * OWN), min(CHIP_BLOCKS, w + 1)):
            at = jnp.clip(w - first[t] + 1, 0, REACH + 1)
            term = parts[t, at]
            total = term if total is None else total + term
        return total * scale_row

    def block(w, count=1):
        return pl.ds(w * BLOCK, count * BLOCK)

    def send_partials(h):
        for w, side, target in ((0, 1, before), (WINDOW - 1, 0, after)):
            s[h][block(w), :] = window_sum(w).astype(jnp.bfloat16)
            away(s[h].at[block(w)], x[h].at[side], x_send.at[h], x_recv.at[h, side],
                 2 * target + core)
        for w in (1, 2, 3, 10, 11, 12):
            s[h][block(w), :] = window_sum(w).astype(jnp.bfloat16)
        from_left, from_right = core, 2 + core
        away(s[h].at[block(1, 2)], r[h].at[from_right], r_send.at[h],
             r_recv.at[h, from_right], 2 * before)
        away(s[h].at[block(11, 2)], r[h].at[from_left], r_send.at[h],
             r_recv.at[h, from_left], 2 * after + 1)
        away(s[h].at[block(3)], r[h].at[from_right, pl.ds(0, BLOCK)], r_send.at[h],
             r_recv.at[h, from_right], 2 * before + 1)
        away(s[h].at[block(10)], r[h].at[from_left, pl.ds(BLOCK, BLOCK)], r_send.at[h],
             r_recv.at[h, from_left], 2 * after)
        edge[h, 0] = window_sum(OWN - 1)
        edge[h, 1] = window_sum(RIGHT)
        for w in range(OWN, RIGHT):
            s[h][block(w), :] = window_sum(w).astype(jnp.bfloat16)
        theirs = pl.ds(pl.multiple_of((OWN + 2 * other) * BLOCK, BLOCK), rows)
        away(s[h].at[theirs], p[h], p_send.at[h], p_recv.at[h], peer)

    def send_edges(h):
        from_left, from_right = core, 2 + core
        wait(x[h].at[1], x_recv.at[h, 1])
        s[h][block(OWN - 1), :] = (edge[h, 0] + x[h][1].astype(jnp.float32)).astype(jnp.bfloat16)
        away(s[h].at[block(OWN - 1)], r[h].at[from_right, pl.ds(BLOCK, BLOCK)], r_send.at[h],
             r_recv.at[h, from_right], 2 * before + 1)
        wait(x[h].at[0], x_recv.at[h, 0])
        s[h][block(RIGHT), :] = (edge[h, 1] + x[h][0].astype(jnp.float32)).astype(jnp.bfloat16)
        away(s[h].at[block(RIGHT)], r[h].at[from_left, pl.ds(0, BLOCK)], r_send.at[h],
             r_recv.at[h, from_left], 2 * after)

    def send_outputs(h):
        at = head_columns(HEADS * core + h, cols)
        for src, dst in ((o[h], o_hbm), (dq[h], dq_hbm)):
            away(src.at[peer_rows], dst.at[:, at], o_send.at[h], o_recv.at[h], peer)
            pltpu.make_async_copy(src.at[token_rows], dst.at[:, at], o_own.at[h]).start()

    for h in range(HEADS):
        send_inputs(h)

    zeros = jnp.zeros((BLOCK, 2 * WIDTH), jnp.float32)
    for t in range(CHIP_BLOCKS):
        parts[t, 0] = zeros
        parts[t, REACH + 1] = zeros
    base = chip * CHIP_BLOCKS
    begins, counts = [base + t for t in range(CHIP_BLOCKS)], [1] * CHIP_BLOCKS
    end = jnp.int32(0)
    for i in range(lengths.shape[0]):
        begin, end = end, end + lengths[i]
        for t in range(CHIP_BLOCKS):
            inside = (begin <= base + t) & (base + t < end)
            shown = jnp.where(fulls[i] > 0, end - begin, base + t - begin + 1)
            begins[t] = jnp.where(inside, begin, begins[t])
            counts[t] = jnp.where(inside, shown, counts[t])
    for t in range(CHIP_BLOCKS):
        first[t] = jnp.clip(begins[t] - base + OWN, t, t + OWN)
        seen[t] = counts[t]

    forward(0)
    wait_inputs(0)
    tiles(0, 0, CHIP_BLOCKS - 1)
    forward(1)
    tiles(0, CHIP_BLOCKS - 1, CHIP_BLOCKS)
    send_partials(0)
    send_outputs(0)
    wait_inputs(1)
    tiles(1, 0, 1)
    send_edges(0)
    tiles(1, 1, CHIP_BLOCKS)
    send_partials(1)
    send_outputs(1)
    send_edges(1)

    for h in range(HEADS):
        wait(p[h], p_recv.at[h])
        for slot in range(4):
            wait(r[h].at[slot], r_recv.at[h, slot])
        own_rows = pl.ds(pl.multiple_of((OWN + 2 * core) * BLOCK, BLOCK), rows)
        for source in (0, 1):
            own = jnp.where(core == source, s[h][own_rows, :].astype(jnp.float32),
                            p[h][...].astype(jnp.float32))
            total = own + r[h][source].astype(jnp.float32) + r[h][2 + source].astype(jnp.float32)
            total = total.astype(jnp.bfloat16)
            at = pl.ds((HEADS * source + h) * WIDTH, WIDTH)
            dk_out[:, at] = total[:, :WIDTH]
            dv_out[:, at] = total[:, WIDTH:]

    for h in range(HEADS):
        wait(q[h].at[:, pl.ds(0, 5 * WIDTH)], kv_send.at[h])
        wait(q[h], q_send.at[h])
        wait(k[h].at[:4], f_send.at[h])
        wait(s[h].at[:rows], x_send.at[h])
        wait(s[h].at[: 4 * rows], r_send.at[h])
        wait(p[h], p_send.at[h])
        wait(o[h], o_own.at[h])
        wait(o[h], o_send.at[h])
        wait(o[h], o_recv.at[h])


def per_device(queries, key_vectors, value_matrix, out_grad, clip_lengths, clip_full):
    local, wide = queries.shape
    narrow = key_vectors.shape[1]
    cols = wide // narrow * WIDTH
    low = jnp.bfloat16
    whole = pl.BlockSpec(memory_space=pltpu.HBM)
    scalars = pl.BlockSpec(memory_space=pltpu.SMEM)
    near = pl.BlockSpec(memory_space=pltpu.VMEM)

    def pair(shape, dtype):
        return [pltpu.VMEM(shape, dtype)] * HEADS

    dma = pltpu.SemaphoreType.DMA
    return pl.pallas_call(
        kernel,
        out_shape=(
            jax.ShapeDtypeStruct((local, wide), low),
            jax.ShapeDtypeStruct((local, wide), low),
            jax.ShapeDtypeStruct((local, narrow), low),
            jax.ShapeDtypeStruct((local, narrow), low),
        ),
        in_specs=[whole] * 4 + [scalars] * 2,
        out_specs=(whole, whole, near, near),
        scratch_shapes=[
            *pair((2 * local, cols), low),
            *pair((2 * local, cols), low),
            *pair((WINDOW, BLOCK, WIDTH), low),
            *pair((WINDOW, BLOCK, WIDTH), low),
            *pair((2 * local, cols), low),
            *pair((2 * local, cols), low),
            pltpu.VMEM((CHIP_BLOCKS, REACH + 2, BLOCK, 2 * WIDTH), jnp.float32),
            *pair((WINDOW * BLOCK, 2 * WIDTH), low),
            pltpu.VMEM((HEADS, 2, BLOCK, 2 * WIDTH), jnp.float32),
            *pair((2, BLOCK, 2 * WIDTH), low),
            *pair((4, local, 2 * WIDTH), low),
            *pair((local, 2 * WIDTH), low),
            pltpu.SMEM((CHIP_BLOCKS,), jnp.int32),
            pltpu.SMEM((CHIP_BLOCKS,), jnp.int32),
            dma((HEADS,)), dma((HEADS, 5)), dma((HEADS,)), dma((HEADS,)),
            dma((HEADS,)), dma((HEADS,)), dma((HEADS,)), dma((HEADS, 2)),
            dma((HEADS,)), dma((HEADS, 2)), dma((HEADS,)), dma((HEADS, 4)),
            dma((HEADS,)), dma((HEADS,)), dma((HEADS,)), dma((HEADS,)), dma((HEADS,)),
        ],
        compiler_params=pltpu.CompilerParams(
            collective_id=0, has_side_effects=True, vmem_limit_bytes=56 * 2**20
        ),
        cost_estimate=pl.CostEstimate(
            flops=12 * local * wide * SPAN,
            bytes_accessed=8 * local * (wide + narrow),
            transcendentals=local * wide // WIDTH * SPAN,
        ),
    )(
        queries,
        key_vectors.reshape(-1, BLOCK, narrow),
        value_matrix.reshape(-1, BLOCK, narrow),
        out_grad,
        clip_lengths,
        clip_full,
    )


def solution(mesh):
    sharded = P(("dp", "ctx"), None)
    return jax.shard_map(
        per_device,
        mesh=mesh,
        in_specs=(sharded, sharded, sharded, sharded, P("dp"), P("dp")),
        out_specs=(sharded, sharded, sharded, sharded),
        check_vma=False,
    )
```

```python
import jax
import jax.numpy as jnp
from jax import lax
from jax.experimental import pallas as pl
from jax.experimental.pallas import tpu as pltpu
from jax.sharding import PartitionSpec as P

MESH = pl.DeviceIdType.MESH
WIDTH = 128
BLOCK = 64
REACH = 6
CHIP_BLOCKS = 4
WINDOW = CHIP_BLOCKS + 2 * (REACH - 1)
OWN = REACH - 1
LEFT = OWN - CHIP_BLOCKS
RIGHT = OWN + CHIP_BLOCKS
HEADS = 2
SPAN = REACH * BLOCK
PIECES = 2
LOG2E = 1.4426950408889634


def kernel(
    q_hbm, k_hbm, v_hbm, g_hbm, lengths, fulls,
    o_hbm, dq_hbm, dk_out, dv_out,
    k_in, v_in, staged, qg_in, qg, kv0, kv1, od, od_far, parts, s0, s1, r0, r1, first, seen,
    kv_in, qg_in_sem, qg_own, kv_send, kv_recv, qg_send, qg_recv,
    r_send, r_recv, o_own, o_send, o_recv, o_far,
):
    kv, s, r = (kv0, kv1), (s0, s1), (r0, r1)
    rows = 2 * BLOCK
    wide = qg.shape[2]
    cols = wide // HEADS
    group = cols // WIDTH
    me, row = lax.axis_index("ctx"), lax.axis_index("dp")
    chips = lax.axis_size("ctx") // 2
    chip, core = me // 2, lax.rem(me, 2)
    other = 1 - core
    after, after2 = (lax.rem(chip + n, chips) for n in (1, 2))
    before, before2 = (lax.rem(chip + chips - n, chips) for n in (1, 2))
    peer = 2 * chip + other

    def away(src, dst, send, recv, target):
        pltpu.make_async_remote_copy(
            src_ref=src, dst_ref=dst, send_sem=send, recv_sem=recv,
            device_id=(target, row), device_id_type=MESH,
        ).start()

    def near(src, dst, sem):
        pltpu.make_async_copy(src, dst, sem).start()

    def wait(ref, sem):
        pltpu.make_async_copy(ref, ref, sem).wait()

    two_off = jnp.where(core == 0, before2, after2)
    barrier = pltpu.get_barrier_semaphore()
    for device in (
        peer, 2 * before, 2 * before + 1, 2 * after, 2 * after + 1,
        2 * two_off, 2 * two_off + 1, jnp.where(core == 0, 2 * after2, 2 * before2 + 1),
    ):
        pl.semaphore_signal(barrier, inc=1, device_id=(device, row), device_id_type=MESH)

    own_blocks = pl.ds(OWN + 2 * core, 2)
    in_after = pl.ds(LEFT + 2 * core, 2)
    in_before = pl.ds(RIGHT + 2 * core, 2)
    token_rows = pl.ds(pl.multiple_of(core * rows, rows), rows)
    peer_rows = pl.ds(pl.multiple_of(other * rows, rows), rows)
    own_rows = pl.ds(pl.multiple_of((OWN + 2 * core) * BLOCK, BLOCK), rows)
    their_rows = pl.ds(pl.multiple_of((OWN + 2 * other) * BLOCK, BLOCK), rows)
    mine = pl.ds(pl.multiple_of(core * wide, WIDTH), wide)
    theirs = pl.ds(pl.multiple_of(other * wide, WIDTH), wide)

    def head_lanes(h):
        return pl.ds(h * cols, cols)

    def send_kv(h):
        for target in (0, 1):
            src = staged.at[HEADS * target + h]
            away(src, kv[h].at[:, in_after], kv_send.at[h], kv_recv.at[h], 2 * after + target)
            away(src, kv[h].at[:, in_before], kv_send.at[h], kv_recv.at[h], 2 * before + target)
            away(src.at[:, core], kv[h].at[:, (WINDOW - 1) * other], kv_send.at[h],
                 kv_recv.at[h], 2 * two_off + target)
        away(staged.at[HEADS * other + h], kv[h].at[:, own_blocks], kv_send.at[h],
             kv_recv.at[h], peer)

    def send_queries(h):
        away(qg_in.at[:, :, head_lanes(h)], qg.at[:, token_rows, head_lanes(h)],
             qg_send, qg_recv.at[h], peer)

    def wait_inputs(h):
        wait(qg.at[:, :rows, head_lanes(h)], qg_recv.at[h])
        wait(kv[h].at[:, : WINDOW - 2], kv_recv.at[h])

    score_scale = WIDTH**-0.5
    across = (((1,), (1,)), ((), ()))
    down = (((0,), (0,)), ((), ()))

    def load(h, t):
        begin = first[t]
        tokens = pl.ds(t * BLOCK, BLOCK)

        def windowed(kind):
            return jnp.concatenate([kv[h][kind, begin + b] for b in range(REACH)], axis=0)

        def stacked(kind):
            return jnp.concatenate(
                [qg[kind, tokens, pl.ds(h * cols + m * WIDTH, WIDTH)] for m in range(group)],
                axis=0,
            )

        return windowed(0), windowed(1), stacked(0), stacked(1)

    def products(h, t):
        keys, values, query, grad = load(h, t)
        scores = lax.dot_general(keys, query, across, preferred_element_type=jnp.float32)
        dprobs = lax.dot_general(values, grad, across, preferred_element_type=jnp.float32)
        return scores, dprobs

    def softmax(t, scores, dprobs):
        count = seen[t]
        bias = [jnp.where(b < count, 0.0, -jnp.inf).astype(jnp.float32) for b in range(REACH)]
        lows, dlows = [], []
        for c in range(scores.shape[1] // WIDTH):
            lanes = slice(c * WIDTH, (c + 1) * WIDTH)
            logits = scores[:, lanes] * (score_scale * LOG2E)
            logits = jnp.concatenate(
                [logits[:BLOCK]]
                + [logits[b * BLOCK : (b + 1) * BLOCK] + bias[b] for b in range(1, REACH)],
                axis=0,
            )
            weight = jnp.exp2(logits - jnp.max(logits, axis=0, keepdims=True))
            probs = weight * (1.0 / jnp.sum(weight, axis=0, keepdims=True))
            lows.append(probs.astype(jnp.bfloat16))
            dprob = dprobs[:, lanes]
            delta = jnp.sum(probs * dprob, axis=0, keepdims=True)
            dlows.append((probs * (dprob - delta)).astype(jnp.bfloat16))
        return jnp.concatenate(lows, axis=1), jnp.concatenate(dlows, axis=1)

    def finish(h, t, low, dscores):
        keys, values, query, grad = load(h, t)
        dkeys = jnp.dot(dscores, query, preferred_element_type=jnp.float32)
        dvalues = jnp.dot(low, grad, preferred_element_type=jnp.float32)
        for b in range(REACH):
            at = slice(b * BLOCK, (b + 1) * BLOCK)
            parts[t, b + 1, :, :WIDTH] = dkeys[at]
            parts[t, b + 1, :, WIDTH:] = dvalues[at]
        attn = lax.dot_general(values, low, down, preferred_element_type=jnp.float32)
        dquery = lax.dot_general(keys, dscores, down, preferred_element_type=jnp.float32)
        attn = attn.astype(jnp.bfloat16).T
        dquery = (dquery * score_scale).astype(jnp.bfloat16).T
        for m in range(group):
            at = pl.ds(h * cols + m * WIDTH, WIDTH)
            tokens = pl.ds(t * BLOCK, BLOCK)
            od[0, tokens, at] = attn[m * BLOCK : (m + 1) * BLOCK]
            od[1, tokens, at] = dquery[m * BLOCK : (m + 1) * BLOCK]

    def tiles(h):
        made = products(h, 0)
        for t in range(CHIP_BLOCKS):
            ready = made
            if t + 1 < CHIP_BLOCKS:
                made = products(h, t + 1)
            finish(h, t, *softmax(t, *ready))

    scale_row = jnp.where(
        lax.broadcasted_iota(jnp.int32, (1, 2 * WIDTH), 1) < WIDTH, score_scale, 1.0
    ).astype(jnp.float32)

    def put_sums(h, *windows):
        for w in windows:
            total = None
            for t in range(max(0, w - 2 * OWN), min(CHIP_BLOCKS, w + 1)):
                term = parts[t, jnp.clip(w - first[t] + 1, 0, REACH + 1)]
                total = term if total is None else total + term
            s[h][pl.ds(w * BLOCK, BLOCK), :] = (total * scale_row).astype(jnp.bfloat16)

    def send_partials(h):
        def part(w, count, slot, target):
            away(s[h].at[pl.ds(w * BLOCK, count * BLOCK)], slot, r_send.at[h], r_recv.at[h],
                 target)

        far = r[h].at[5, pl.ds(pl.multiple_of(core * BLOCK, BLOCK), BLOCK)]
        put_sums(h, 0, WINDOW - 1)
        part(0, 1, far, 2 * before2 + 1)
        part(WINDOW - 1, 1, far, 2 * after2)
        put_sums(h, 1, 2, 9, 10)
        part(LEFT, 2, r[h].at[2 + core], 2 * before)
        part(RIGHT, 2, r[h].at[core], 2 * after)
        put_sums(h, 3, 4, 11, 12)
        part(LEFT + 2, 2, r[h].at[2 + core], 2 * before + 1)
        part(RIGHT + 2, 2, r[h].at[core], 2 * after + 1)
        put_sums(h, *range(OWN, RIGHT))
        away(s[h].at[their_rows], r[h].at[4], r_send.at[h], r_recv.at[h], peer)

    def collect(h):
        wait(r[h], r_recv.at[h])
        nothing = jnp.zeros((BLOCK, 2 * WIDTH), jnp.float32)
        for source in (0, 1):
            own = jnp.where(core == source, s[h][own_rows, :].astype(jnp.float32),
                            r[h][4].astype(jnp.float32))
            far = r[h][5, pl.ds(source * BLOCK, BLOCK)].astype(jnp.float32)
            far = jnp.concatenate(
                [jnp.where(core == 0, far, nothing), jnp.where(core == 1, far, nothing)], axis=0
            )
            total = own + r[h][source].astype(jnp.float32) + r[h][2 + source].astype(jnp.float32)
            total = (total + far).astype(jnp.bfloat16)
            at = pl.ds((HEADS * source + h) * WIDTH, WIDTH)
            dk_out[:, at] = total[:, :WIDTH]
            dv_out[:, at] = total[:, WIDTH:]

    def send_outputs(h):
        away(od.at[:, peer_rows, head_lanes(h)], od_far.at[:, :, head_lanes(h)], o_send,
             o_recv, peer)

    for i, (src, dst) in enumerate(((k_hbm, k_in), (v_hbm, v_in))):
        near(src, dst, kv_in.at[i])
    for i, src in enumerate((q_hbm, g_hbm)):
        near(src.at[:, theirs], qg_in.at[i], qg_in_sem)
        near(src.at[:, mine], qg.at[i, token_rows], qg_own)

    zeros = jnp.zeros((BLOCK, 2 * WIDTH), jnp.float32)
    for t in range(CHIP_BLOCKS):
        parts[t, 0] = zeros
        parts[t, REACH + 1] = zeros
    base = chip * CHIP_BLOCKS
    begins, counts = [base + t for t in range(CHIP_BLOCKS)], [1] * CHIP_BLOCKS
    end = jnp.int32(0)
    for i in range(lengths.shape[0]):
        begin, end = end, end + lengths[i]
        for t in range(CHIP_BLOCKS):
            inside = (begin <= base + t) & (base + t < end)
            shown = jnp.where(fulls[i] > 0, end - begin, base + t - begin + 1)
            begins[t] = jnp.where(inside, begin, begins[t])
            counts[t] = jnp.where(inside, shown, counts[t])
    for t in range(CHIP_BLOCKS):
        first[t] = jnp.clip(begins[t] - base + OWN, t, t + OWN)
        seen[t] = counts[t]

    for kind, held in enumerate((k_in, v_in)):
        wait(held, kv_in.at[kind])
        for head in range(2 * HEADS):
            staged[head, kind] = held[:, :, pl.ds(head * WIDTH, WIDTH)]
    pl.semaphore_wait(barrier, 8)
    send_kv(0)
    wait(qg_in, qg_in_sem)
    send_queries(0)
    send_kv(1)
    send_queries(1)
    for h in range(HEADS):
        for kind in (0, 1):
            kv[h][kind, own_blocks] = staged[HEADS * core + h, kind]
    wait(qg_in, qg_own)

    for h in range(HEADS):
        wait_inputs(h)
        tiles(h)
        send_partials(h)
        send_outputs(h)
    for i, dst in enumerate((o_hbm, dq_hbm)):
        near(od.at[i, token_rows], dst.at[:, mine], o_own)
    collect(0)
    wait(od_far, o_recv)
    for i, dst in enumerate((o_hbm, dq_hbm)):
        near(od_far.at[i], dst.at[:, theirs], o_far)
    collect(1)

    for h in range(HEADS):
        wait(kv[h].at[:, : WINDOW - 2], kv_send.at[h])
        wait(r[h], r_send.at[h])
    wait(qg_in, qg_send)
    wait(od_far, o_send)
    wait(od_far, o_own)
    wait(od_far, o_far)


def settle(*refs):
    refs, (loaded, stored) = refs[:-2], refs[-2:]
    count = len(refs) // 3
    steps = []
    for i in range(count):
        src, dst, held = refs[i], refs[count + i], refs[2 * count + i]
        pieces = PIECES if held.shape == refs[0].shape else 1
        size = held.shape[0] // pieces
        for piece in range(pieces):
            at = pl.ds(piece * size, size)
            load = pltpu.make_async_copy(src.at[at], held.at[at], loaded.at[i, piece])
            store = pltpu.make_async_copy(held.at[at], dst.at[at], stored.at[i, piece])
            load.start()
            steps.append((load, store))
    for load, store in steps:
        load.wait()
        store.start()
    for load, store in steps:
        store.wait()


def per_device(queries, key_vectors, value_matrix, out_grad, clip_lengths, clip_full):
    local, wide = queries.shape
    narrow = key_vectors.shape[1]
    half = wide // 2
    low = jnp.bfloat16
    whole = pl.BlockSpec(memory_space=pltpu.HBM)
    scalars = pl.BlockSpec(memory_space=pltpu.SMEM)
    near = pl.BlockSpec(memory_space=pltpu.VMEM)
    dma = pltpu.SemaphoreType.DMA

    def some(count, shape, dtype=low):
        return [pltpu.VMEM(shape, dtype)] * count

    shapes = [jax.ShapeDtypeStruct((local, n), low) for n in (wide, wide, narrow, narrow)]
    results = pl.pallas_call(
        kernel,
        out_shape=shapes,
        in_specs=[whole] * 4 + [scalars] * 2,
        out_specs=(whole, whole, near, near),
        scratch_shapes=[
            *some(2, (local // BLOCK, BLOCK, narrow)),
            pltpu.VMEM((2 * HEADS, 2, local // BLOCK, BLOCK, WIDTH), low),
            pltpu.VMEM((2, local, half), low),
            pltpu.VMEM((2, 2 * local, half), low),
            *some(HEADS, (2, WINDOW, BLOCK, WIDTH)),
            pltpu.VMEM((2, 2 * local, half), low),
            pltpu.VMEM((2, local, half), low),
            pltpu.VMEM((CHIP_BLOCKS, REACH + 2, BLOCK, 2 * WIDTH), jnp.float32),
            *some(HEADS, (WINDOW * BLOCK, 2 * WIDTH)),
            *some(HEADS, (6, local, 2 * WIDTH)),
            pltpu.SMEM((CHIP_BLOCKS,), jnp.int32),
            pltpu.SMEM((CHIP_BLOCKS,), jnp.int32),
            dma((2,)), dma, dma, dma((HEADS,)), dma((HEADS,)), dma, dma((HEADS,)),
            dma((HEADS,)), dma((HEADS,)), dma, dma, dma, dma,
        ],
        compiler_params=pltpu.CompilerParams(
            collective_id=0, has_side_effects=True, vmem_limit_bytes=56 * 2**20
        ),
        cost_estimate=pl.CostEstimate(
            flops=12 * local * wide * SPAN,
            bytes_accessed=8 * local * (wide + narrow),
            transcendentals=local * wide // WIDTH * SPAN,
        ),
    )(
        queries,
        key_vectors.reshape(-1, BLOCK, narrow),
        value_matrix.reshape(-1, BLOCK, narrow),
        out_grad,
        clip_lengths,
        clip_full,
    )
    return pl.pallas_call(
        settle,
        out_shape=shapes,
        in_specs=[pl.BlockSpec(memory_space=pl.ANY)] * 4,
        out_specs=[whole] * 4,
        scratch_shapes=[
            *some(2, (local, wide)),
            *some(2, (local, narrow)),
            dma((4, PIECES)),
            dma((4, PIECES)),
        ],
        compiler_params=pltpu.CompilerParams(vmem_limit_bytes=56 * 2**20),
    )(*results)


def solution(mesh):
    sharded = P(("dp", "ctx"), None)
    return jax.shard_map(
        per_device,
        mesh=mesh,
        in_specs=(sharded, sharded, sharded, sharded, P("dp"), P("dp")),
        out_specs=(sharded, sharded, sharded, sharded),
        check_vma=False,
    )
```

```python
import jax
import jax.numpy as jnp
from jax import lax
from jax.experimental import pallas as pl
from jax.experimental.pallas import tpu as pltpu
from jax.sharding import PartitionSpec as P

MESH = pl.DeviceIdType.MESH
WIDTH = 128
BLOCK = 64
REACH = 6
CHIP_BLOCKS = 4
WINDOW = CHIP_BLOCKS + 2 * (REACH - 1)
OWN = REACH - 1
LEFT = OWN - CHIP_BLOCKS
RIGHT = OWN + CHIP_BLOCKS
HEADS = 2
SPAN = REACH * BLOCK
PIECES = 2
ORDER = (0, 3, 1, 2)
LOG2E = 1.4426950408889634


def kernel(
    q_hbm, k_hbm, v_hbm, g_hbm, lengths, fulls,
    o_hbm, dq_hbm, dk_out, dv_out,
    k_in, v_in, staged, qg_in, qg, kv0, kv1, od, od_far, parts, low_held, dlow_held, s0, s1, r0, r1,
    first, seen,
    kv_in, qg_in_sem, qg_own, kv_send, kv_recv, qg_send, qg_recv,
    r_send, r_recv, o_own, o_send, o_recv, o_far,
):
    kv, s, r = (kv0, kv1), (s0, s1), (r0, r1)
    rows = 2 * BLOCK
    wide = qg.shape[2]
    cols = wide // HEADS
    group = cols // WIDTH
    me, row = lax.axis_index("ctx"), lax.axis_index("dp")
    chips = lax.axis_size("ctx") // 2
    chip, core = me // 2, lax.rem(me, 2)
    other = 1 - core
    after, after2 = (lax.rem(chip + n, chips) for n in (1, 2))
    before, before2 = (lax.rem(chip + chips - n, chips) for n in (1, 2))
    peer = 2 * chip + other

    def away(src, dst, send, recv, target):
        pltpu.make_async_remote_copy(
            src_ref=src, dst_ref=dst, send_sem=send, recv_sem=recv,
            device_id=(target, row), device_id_type=MESH,
        ).start()

    def near(src, dst, sem):
        pltpu.make_async_copy(src, dst, sem).start()

    def wait(ref, sem):
        pltpu.make_async_copy(ref, ref, sem).wait()

    two_off = jnp.where(core == 0, before2, after2)
    barrier = pltpu.get_barrier_semaphore()
    for device in (
        peer, 2 * before, 2 * before + 1, 2 * after, 2 * after + 1,
        2 * two_off, 2 * two_off + 1, jnp.where(core == 0, 2 * after2, 2 * before2 + 1),
    ):
        pl.semaphore_signal(barrier, inc=1, device_id=(device, row), device_id_type=MESH)

    own_blocks = pl.ds(OWN + 2 * core, 2)
    in_after = pl.ds(LEFT + 2 * core, 2)
    in_before = pl.ds(RIGHT + 2 * core, 2)
    token_rows = pl.ds(pl.multiple_of(core * rows, rows), rows)
    peer_rows = pl.ds(pl.multiple_of(other * rows, rows), rows)
    own_rows = pl.ds(pl.multiple_of((OWN + 2 * core) * BLOCK, BLOCK), rows)
    their_rows = pl.ds(pl.multiple_of((OWN + 2 * other) * BLOCK, BLOCK), rows)
    mine = pl.ds(pl.multiple_of(core * wide, WIDTH), wide)
    theirs = pl.ds(pl.multiple_of(other * wide, WIDTH), wide)

    def head_lanes(h):
        return pl.ds(h * cols, cols)

    def send_kv(h):
        for target in (0, 1):
            src = staged.at[HEADS * target + h]
            away(src.at[:, core], kv[h].at[:, (WINDOW - 1) * other], kv_send.at[h],
                 kv_recv.at[h], 2 * two_off + target)
            away(src, kv[h].at[:, in_after], kv_send.at[h], kv_recv.at[h], 2 * after + target)
            away(src, kv[h].at[:, in_before], kv_send.at[h], kv_recv.at[h], 2 * before + target)
        away(staged.at[HEADS * other + h], kv[h].at[:, own_blocks], kv_send.at[h],
             kv_recv.at[h], peer)

    def send_queries(h):
        away(qg_in.at[:, :, head_lanes(h)], qg.at[:, token_rows, head_lanes(h)],
             qg_send, qg_recv.at[h], peer)

    def wait_inputs(h):
        wait(qg.at[:, :rows, head_lanes(h)], qg_recv.at[h])
        wait(kv[h].at[:, : WINDOW - 2], kv_recv.at[h])

    score_scale = WIDTH**-0.5
    across = (((1,), (1,)), ((), ()))
    down = (((0,), (0,)), ((), ()))

    def load(h, t):
        begin = first[t]
        tokens = pl.ds(t * BLOCK, BLOCK)

        def windowed(kind):
            return jnp.concatenate([kv[h][kind, begin + b] for b in range(REACH)], axis=0)

        def stacked(kind):
            return jnp.concatenate(
                [qg[kind, tokens, pl.ds(h * cols + m * WIDTH, WIDTH)] for m in range(group)],
                axis=0,
            )

        return windowed(0), windowed(1), stacked(0), stacked(1)

    def products(h, t):
        keys, values, query, grad = load(h, t)
        scores = lax.dot_general(keys, query, across, preferred_element_type=jnp.float32)
        dprobs = lax.dot_general(values, grad, across, preferred_element_type=jnp.float32)
        return scores, dprobs

    def softmax(t, scores, dprobs):
        count = seen[t]
        bias = [jnp.where(b < count, 0.0, -jnp.inf).astype(jnp.float32) for b in range(REACH)]
        lows, dlows = [], []
        for c in range(scores.shape[1] // WIDTH):
            lanes = slice(c * WIDTH, (c + 1) * WIDTH)
            logits = scores[:, lanes] * (score_scale * LOG2E)
            logits = jnp.concatenate(
                [logits[:BLOCK]]
                + [logits[b * BLOCK : (b + 1) * BLOCK] + bias[b] for b in range(1, REACH)],
                axis=0,
            )
            weight = jnp.exp2(logits - jnp.max(logits, axis=0, keepdims=True))
            probs = weight * (1.0 / jnp.sum(weight, axis=0, keepdims=True))
            lows.append(probs.astype(jnp.bfloat16))
            dprob = dprobs[:, lanes]
            delta = jnp.sum(probs * dprob, axis=0, keepdims=True)
            dlows.append((probs * (dprob - delta)).astype(jnp.bfloat16))
        return jnp.concatenate(lows, axis=1), jnp.concatenate(dlows, axis=1)

    def finish(h, t, low, dscores):
        _, _, query, grad = load(h, t)
        low_held[t] = low
        dlow_held[t] = dscores
        dkeys = jnp.dot(dscores, query, preferred_element_type=jnp.float32)
        dvalues = jnp.dot(low, grad, preferred_element_type=jnp.float32)
        for b in range(REACH):
            at = slice(b * BLOCK, (b + 1) * BLOCK)
            parts[t, b + 1, :, :WIDTH] = dkeys[at]
            parts[t, b + 1, :, WIDTH:] = dvalues[at]

    def tiles(h):
        made = products(h, ORDER[0])
        for i, t in enumerate(ORDER):
            ready = made
            if i + 1 < CHIP_BLOCKS:
                made = products(h, ORDER[i + 1])
            finish(h, t, *softmax(t, *ready))
            if t == 0:
                put_sums(h, 0)
                part(h, 0, 1, far_slot(h), 2 * before2 + 1)
            if t == CHIP_BLOCKS - 1:
                put_sums(h, WINDOW - 1)
                part(h, WINDOW - 1, 1, far_slot(h), 2 * after2)

    def outputs(h):
        for t in range(CHIP_BLOCKS):
            keys, values, _, _ = load(h, t)
            attn = lax.dot_general(values, low_held[t], down, preferred_element_type=jnp.float32)
            dquery = lax.dot_general(keys, dlow_held[t], down, preferred_element_type=jnp.float32)
            attn = attn.astype(jnp.bfloat16).T
            dquery = (dquery * score_scale).astype(jnp.bfloat16).T
            for m in range(group):
                at = pl.ds(h * cols + m * WIDTH, WIDTH)
                tokens = pl.ds(t * BLOCK, BLOCK)
                od[0, tokens, at] = attn[m * BLOCK : (m + 1) * BLOCK]
                od[1, tokens, at] = dquery[m * BLOCK : (m + 1) * BLOCK]

    scale_row = jnp.where(
        lax.broadcasted_iota(jnp.int32, (1, 2 * WIDTH), 1) < WIDTH, score_scale, 1.0
    ).astype(jnp.float32)

    def put_sums(h, *windows):
        for w in windows:
            total = None
            for t in range(max(0, w - 2 * OWN), min(CHIP_BLOCKS, w + 1)):
                term = parts[t, jnp.clip(w - first[t] + 1, 0, REACH + 1)]
                total = term if total is None else total + term
            s[h][pl.ds(w * BLOCK, BLOCK), :] = (total * scale_row).astype(jnp.bfloat16)

    def part(h, w, count, slot, target):
        away(s[h].at[pl.ds(w * BLOCK, count * BLOCK)], slot, r_send.at[h], r_recv.at[h], target)

    def far_slot(h):
        return r[h].at[5, pl.ds(pl.multiple_of(core * BLOCK, BLOCK), BLOCK)]

    def send_partials(h):
        put_sums(h, 1, 2, 9, 10)
        part(h, LEFT, 2, r[h].at[2 + core], 2 * before)
        part(h, RIGHT, 2, r[h].at[core], 2 * after)
        put_sums(h, 3, 4, 11, 12)
        part(h, LEFT + 2, 2, r[h].at[2 + core], 2 * before + 1)
        part(h, RIGHT + 2, 2, r[h].at[core], 2 * after + 1)
        put_sums(h, *range(OWN, RIGHT))
        away(s[h].at[their_rows], r[h].at[4], r_send.at[h], r_recv.at[h], peer)

    def collect(h):
        wait(r[h], r_recv.at[h])
        nothing = jnp.zeros((BLOCK, 2 * WIDTH), jnp.float32)
        for source in (0, 1):
            own = jnp.where(core == source, s[h][own_rows, :].astype(jnp.float32),
                            r[h][4].astype(jnp.float32))
            far = r[h][5, pl.ds(source * BLOCK, BLOCK)].astype(jnp.float32)
            far = jnp.concatenate(
                [jnp.where(core == 0, far, nothing), jnp.where(core == 1, far, nothing)], axis=0
            )
            total = own + r[h][source].astype(jnp.float32) + r[h][2 + source].astype(jnp.float32)
            total = (total + far).astype(jnp.bfloat16)
            at = pl.ds((HEADS * source + h) * WIDTH, WIDTH)
            dk_out[:, at] = total[:, :WIDTH]
            dv_out[:, at] = total[:, WIDTH:]

    def send_outputs(h):
        away(od.at[:, peer_rows, head_lanes(h)], od_far.at[:, :, head_lanes(h)], o_send,
             o_recv, peer)

    for i, (src, dst) in enumerate(((k_hbm, k_in), (v_hbm, v_in))):
        near(src, dst, kv_in.at[i])
    for i, src in enumerate((q_hbm, g_hbm)):
        near(src.at[:, theirs], qg_in.at[i], qg_in_sem)
        near(src.at[:, mine], qg.at[i, token_rows], qg_own)

    zeros = jnp.zeros((BLOCK, 2 * WIDTH), jnp.float32)
    for t in range(CHIP_BLOCKS):
        parts[t, 0] = zeros
        parts[t, REACH + 1] = zeros
    base = chip * CHIP_BLOCKS
    begins, counts = [base + t for t in range(CHIP_BLOCKS)], [1] * CHIP_BLOCKS
    end = jnp.int32(0)
    for i in range(lengths.shape[0]):
        begin, end = end, end + lengths[i]
        for t in range(CHIP_BLOCKS):
            inside = (begin <= base + t) & (base + t < end)
            shown = jnp.where(fulls[i] > 0, end - begin, base + t - begin + 1)
            begins[t] = jnp.where(inside, begin, begins[t])
            counts[t] = jnp.where(inside, shown, counts[t])
    for t in range(CHIP_BLOCKS):
        first[t] = jnp.clip(begins[t] - base + OWN, t, t + OWN)
        seen[t] = counts[t]

    for kind, held in enumerate((k_in, v_in)):
        wait(held, kv_in.at[kind])
        for head in range(2 * HEADS):
            staged[head, kind] = held[:, :, pl.ds(head * WIDTH, WIDTH)]
    pl.semaphore_wait(barrier, 8)
    send_kv(0)
    wait(qg_in, qg_in_sem)
    send_queries(0)
    for h in range(HEADS):
        for kind in (0, 1):
            kv[h][kind, own_blocks] = staged[HEADS * core + h, kind]
    wait(qg_in, qg_own)

    for h in range(HEADS):
        wait_inputs(h)
        if h + 1 < HEADS:
            send_kv(h + 1)
            send_queries(h + 1)
        tiles(h)
        send_partials(h)
        outputs(h)
        send_outputs(h)
    for i, dst in enumerate((o_hbm, dq_hbm)):
        near(od.at[i, token_rows], dst.at[:, mine], o_own)
    collect(0)
    wait(od_far, o_recv)
    for i, dst in enumerate((o_hbm, dq_hbm)):
        near(od_far.at[i], dst.at[:, theirs], o_far)
    collect(1)

    for h in range(HEADS):
        wait(kv[h].at[:, : WINDOW - 2], kv_send.at[h])
        wait(r[h], r_send.at[h])
    wait(qg_in, qg_send)
    wait(od_far, o_send)
    wait(od_far, o_own)
    wait(od_far, o_far)


def settle(*refs):
    refs, (loaded, stored) = refs[:-2], refs[-2:]
    count = len(refs) // 3
    steps = []
    for i in range(count):
        src, dst, held = refs[i], refs[count + i], refs[2 * count + i]
        pieces = PIECES if held.shape == refs[0].shape else 1
        size = held.shape[0] // pieces
        for piece in range(pieces):
            at = pl.ds(piece * size, size)
            load = pltpu.make_async_copy(src.at[at], held.at[at], loaded.at[i, piece])
            store = pltpu.make_async_copy(held.at[at], dst.at[at], stored.at[i, piece])
            load.start()
            steps.append((load, store))
    for load, store in steps:
        load.wait()
        store.start()
    for load, store in steps:
        store.wait()


def per_device(queries, key_vectors, value_matrix, out_grad, clip_lengths, clip_full):
    local, wide = queries.shape
    narrow = key_vectors.shape[1]
    half = wide // 2
    low = jnp.bfloat16
    whole = pl.BlockSpec(memory_space=pltpu.HBM)
    scalars = pl.BlockSpec(memory_space=pltpu.SMEM)
    near = pl.BlockSpec(memory_space=pltpu.VMEM)
    dma = pltpu.SemaphoreType.DMA

    def some(count, shape, dtype=low):
        return [pltpu.VMEM(shape, dtype)] * count

    shapes = [jax.ShapeDtypeStruct((local, n), low) for n in (wide, wide, narrow, narrow)]
    results = pl.pallas_call(
        kernel,
        out_shape=shapes,
        in_specs=[whole] * 4 + [scalars] * 2,
        out_specs=(whole, whole, near, near),
        scratch_shapes=[
            *some(2, (local // BLOCK, BLOCK, narrow)),
            pltpu.VMEM((2 * HEADS, 2, local // BLOCK, BLOCK, WIDTH), low),
            pltpu.VMEM((2, local, half), low),
            pltpu.VMEM((2, 2 * local, half), low),
            *some(HEADS, (2, WINDOW, BLOCK, WIDTH)),
            pltpu.VMEM((2, 2 * local, half), low),
            pltpu.VMEM((2, local, half), low),
            pltpu.VMEM((CHIP_BLOCKS, REACH + 2, BLOCK, 2 * WIDTH), jnp.float32),
            *some(2, (CHIP_BLOCKS, SPAN, half // HEADS // WIDTH * BLOCK)),
            *some(HEADS, (WINDOW * BLOCK, 2 * WIDTH)),
            *some(HEADS, (6, local, 2 * WIDTH)),
            pltpu.SMEM((CHIP_BLOCKS,), jnp.int32),
            pltpu.SMEM((CHIP_BLOCKS,), jnp.int32),
            dma((2,)), dma, dma, dma((HEADS,)), dma((HEADS,)), dma, dma((HEADS,)),
            dma((HEADS,)), dma((HEADS,)), dma, dma, dma, dma,
        ],
        compiler_params=pltpu.CompilerParams(
            collective_id=0, has_side_effects=True, vmem_limit_bytes=56 * 2**20
        ),
        cost_estimate=pl.CostEstimate(
            flops=12 * local * wide * SPAN,
            bytes_accessed=8 * local * (wide + narrow),
            transcendentals=local * wide // WIDTH * SPAN,
        ),
    )(
        queries,
        key_vectors.reshape(-1, BLOCK, narrow),
        value_matrix.reshape(-1, BLOCK, narrow),
        out_grad,
        clip_lengths,
        clip_full,
    )
    return pl.pallas_call(
        settle,
        out_shape=shapes,
        in_specs=[pl.BlockSpec(memory_space=pl.ANY)] * 4,
        out_specs=[whole] * 4,
        scratch_shapes=[
            *some(2, (local, wide)),
            *some(2, (local, narrow)),
            dma((4, PIECES)),
            dma((4, PIECES)),
        ],
        compiler_params=pltpu.CompilerParams(vmem_limit_bytes=56 * 2**20),
    )(*results)


def solution(mesh):
    sharded = P(("dp", "ctx"), None)
    return jax.shard_map(
        per_device,
        mesh=mesh,
        in_specs=(sharded, sharded, sharded, sharded, P("dp"), P("dp")),
        out_specs=(sharded, sharded, sharded, sharded),
        check_vma=False,
    )
```

```python
import jax
import jax.numpy as jnp
from jax import lax
from jax.experimental import pallas as pl
from jax.experimental.pallas import tpu as pltpu
from jax.sharding import PartitionSpec as P

MESH = pl.DeviceIdType.MESH
WIDTH = 128
BLOCK = 64
REACH = 6
CHIP_BLOCKS = 4
WINDOW = CHIP_BLOCKS + 2 * (REACH - 1)
OWN = REACH - 1
LEFT = OWN - CHIP_BLOCKS
RIGHT = OWN + CHIP_BLOCKS
HEADS = 2
SPAN = REACH * BLOCK
PIECES = 2
LOG2E = 1.4426950408889634


def kernel(
    q_hbm, k_hbm, v_hbm, g_hbm, lengths, fulls,
    o_hbm, dq_hbm, dk_out, dv_out,
    k_in, v_in, staged, qg_in, qg, kv0, kv1, od, od_far, parts, s0, s1, r0, r1, first, seen,
    kv_in, qg_in_sem, qg_own, kv_send, kv_recv, qg_send, qg_recv,
    r_send, r_recv, o_own, o_send, o_recv, o_far,
):
    kv, s, r = (kv0, kv1), (s0, s1), (r0, r1)
    rows = 2 * BLOCK
    wide = qg.shape[2]
    cols = wide // HEADS
    group = cols // WIDTH
    me, row = lax.axis_index("ctx"), lax.axis_index("dp")
    chips = lax.axis_size("ctx") // 2
    chip, core = me // 2, lax.rem(me, 2)
    other = 1 - core
    after, after2 = (lax.rem(chip + n, chips) for n in (1, 2))
    before, before2 = (lax.rem(chip + chips - n, chips) for n in (1, 2))
    peer = 2 * chip + other

    def away(src, dst, send, recv, target):
        pltpu.make_async_remote_copy(
            src_ref=src, dst_ref=dst, send_sem=send, recv_sem=recv,
            device_id=(target, row), device_id_type=MESH,
        ).start()

    def near(src, dst, sem):
        pltpu.make_async_copy(src, dst, sem).start()

    def wait(ref, sem):
        pltpu.make_async_copy(ref, ref, sem).wait()

    two_off = jnp.where(core == 0, before2, after2)
    barrier = pltpu.get_barrier_semaphore()
    for device in (
        peer, 2 * before, 2 * before + 1, 2 * after, 2 * after + 1,
        2 * two_off, 2 * two_off + 1, jnp.where(core == 0, 2 * after2, 2 * before2 + 1),
    ):
        pl.semaphore_signal(barrier, inc=1, device_id=(device, row), device_id_type=MESH)

    own_blocks = pl.ds(OWN + 2 * core, 2)
    in_after = pl.ds(LEFT + 2 * core, 2)
    in_before = pl.ds(RIGHT + 2 * core, 2)
    token_rows = pl.ds(pl.multiple_of(core * rows, rows), rows)
    peer_rows = pl.ds(pl.multiple_of(other * rows, rows), rows)
    own_rows = pl.ds(pl.multiple_of((OWN + 2 * core) * BLOCK, BLOCK), rows)
    their_rows = pl.ds(pl.multiple_of((OWN + 2 * other) * BLOCK, BLOCK), rows)
    mine = pl.ds(pl.multiple_of(core * wide, WIDTH), wide)
    theirs = pl.ds(pl.multiple_of(other * wide, WIDTH), wide)

    def head_lanes(h):
        return pl.ds(h * cols, cols)

    def send_kv(h):
        for target in (0, 1):
            src = staged.at[HEADS * target + h]
            away(src, kv[h].at[:, in_after], kv_send.at[h], kv_recv.at[h], 2 * after + target)
            away(src, kv[h].at[:, in_before], kv_send.at[h], kv_recv.at[h], 2 * before + target)
            away(src.at[:, core], kv[h].at[:, (WINDOW - 1) * other], kv_send.at[h],
                 kv_recv.at[h], 2 * two_off + target)
        away(staged.at[HEADS * other + h], kv[h].at[:, own_blocks], kv_send.at[h],
             kv_recv.at[h], peer)

    def send_queries(h):
        away(qg_in.at[:, :, head_lanes(h)], qg.at[:, token_rows, head_lanes(h)],
             qg_send, qg_recv.at[h], peer)

    def wait_inputs(h):
        wait(qg.at[:, :rows, head_lanes(h)], qg_recv.at[h])
        wait(kv[h].at[:, : WINDOW - 2], kv_recv.at[h])

    score_scale = WIDTH**-0.5
    across = (((1,), (1,)), ((), ()))
    down = (((0,), (0,)), ((), ()))

    def windowed(h, kind, t):
        begin = first[t]
        return jnp.concatenate([kv[h][kind, begin + b] for b in range(REACH)], axis=0)

    def stacked(h, kind, t, members):
        tokens = pl.ds(t * BLOCK, BLOCK)
        return jnp.concatenate(
            [qg[kind, tokens, pl.ds(h * cols + m * WIDTH, WIDTH)] for m in members], axis=0
        )

    def tiles(h):
        work = [
            (t, members)
            for t in range(CHIP_BLOCKS)
            for members in (range(0, 4), range(4, group))
        ]
        made, soft, sums = {}, {}, {}

        def products(i):
            t, members = work[i]

            def step(kind):
                def run():
                    made[i, kind] = lax.dot_general(
                        windowed(h, kind, t), stacked(h, kind, t, members), across,
                        preferred_element_type=jnp.float32,
                    )

                return run

            return [step(0), step(1)]

        def softmax(i):
            t, members = work[i]
            soft[i] = ([], [])

            def step(c):
                def run():
                    count = seen[t]
                    lanes = slice(c * WIDTH, (c + 1) * WIDTH)
                    logits = made[i, 0][:, lanes] * (score_scale * LOG2E)
                    pieces = [logits[:BLOCK]]
                    for b in range(1, REACH):
                        bias = jnp.where(b < count, 0.0, -jnp.inf).astype(jnp.float32)
                        pieces.append(logits[b * BLOCK : (b + 1) * BLOCK] + bias)
                    logits = jnp.concatenate(pieces, axis=0)
                    weight = jnp.exp2(logits - jnp.max(logits, axis=0, keepdims=True))
                    probs = weight * (1.0 / jnp.sum(weight, axis=0, keepdims=True))
                    soft[i][0].append(probs.astype(jnp.bfloat16))
                    dprob = made[i, 1][:, lanes]
                    delta = jnp.sum(probs * dprob, axis=0, keepdims=True)
                    soft[i][1].append((probs * (dprob - delta)).astype(jnp.bfloat16))

                return run

            return [step(c) for c in range(len(members) * BLOCK // WIDTH)]

        def gradients(i):
            t, members = work[i]

            def to_keys(kind):
                def run():
                    inner = jnp.concatenate(soft[i][1 - kind], axis=1)
                    sums[i, kind] = jnp.dot(inner, stacked(h, kind, t, members),
                                            preferred_element_type=jnp.float32)
                    if i % 2:
                        total = sums[i - 1, kind] + sums[i, kind]
                        for b in range(REACH):
                            parts[t, b + 1, :, pl.ds(kind * WIDTH, WIDTH)] = (
                                total[b * BLOCK : (b + 1) * BLOCK]
                            )

                return run

            def to_queries(kind):
                def run():
                    inner = jnp.concatenate(soft[i][1 - kind], axis=1)
                    found = lax.dot_general(windowed(h, kind, t), inner, down,
                                            preferred_element_type=jnp.float32)
                    if kind == 0:
                        found = found * score_scale
                    found = found.astype(jnp.bfloat16).T
                    for n, m in enumerate(members):
                        od[1 - kind, pl.ds(t * BLOCK, BLOCK), pl.ds(h * cols + m * WIDTH, WIDTH)] = (
                            found[n * BLOCK : (n + 1) * BLOCK]
                        )

                return run

            return [to_keys(0), to_keys(1), to_queries(0), to_queries(1)]

        for i in range(-1, len(work) + 1):
            stages = [
                gradients(i - 1) if 0 < i else [],
                softmax(i) if 0 <= i < len(work) else [],
                products(i + 1) if i + 1 < len(work) else [],
            ]
            longest = max(len(stage) for stage in stages)
            for n in range(longest):
                for stage in stages:
                    for step in stage[n * len(stage) // longest : (n + 1) * len(stage) // longest]:
                        step()

    scale_row = jnp.where(
        lax.broadcasted_iota(jnp.int32, (1, 2 * WIDTH), 1) < WIDTH, score_scale, 1.0
    ).astype(jnp.float32)

    def put_sums(h, *windows):
        for w in windows:
            total = None
            for t in range(max(0, w - 2 * OWN), min(CHIP_BLOCKS, w + 1)):
                term = parts[t, jnp.clip(w - first[t] + 1, 0, REACH + 1)]
                total = term if total is None else total + term
            s[h][pl.ds(w * BLOCK, BLOCK), :] = (total * scale_row).astype(jnp.bfloat16)

    def send_partials(h):
        def part(w, count, slot, target):
            away(s[h].at[pl.ds(w * BLOCK, count * BLOCK)], slot, r_send.at[h], r_recv.at[h],
                 target)

        far = r[h].at[5, pl.ds(pl.multiple_of(core * BLOCK, BLOCK), BLOCK)]
        put_sums(h, 0, WINDOW - 1)
        part(0, 1, far, 2 * before2 + 1)
        part(WINDOW - 1, 1, far, 2 * after2)
        put_sums(h, 1, 2, 9, 10)
        part(LEFT, 2, r[h].at[2 + core], 2 * before)
        part(RIGHT, 2, r[h].at[core], 2 * after)
        put_sums(h, 3, 4, 11, 12)
        part(LEFT + 2, 2, r[h].at[2 + core], 2 * before + 1)
        part(RIGHT + 2, 2, r[h].at[core], 2 * after + 1)
        put_sums(h, *range(OWN, RIGHT))
        away(s[h].at[their_rows], r[h].at[4], r_send.at[h], r_recv.at[h], peer)

    def collect(h):
        wait(r[h], r_recv.at[h])
        nothing = jnp.zeros((BLOCK, 2 * WIDTH), jnp.float32)
        for source in (0, 1):
            own = jnp.where(core == source, s[h][own_rows, :].astype(jnp.float32),
                            r[h][4].astype(jnp.float32))
            far = r[h][5, pl.ds(source * BLOCK, BLOCK)].astype(jnp.float32)
            far = jnp.concatenate(
                [jnp.where(core == 0, far, nothing), jnp.where(core == 1, far, nothing)], axis=0
            )
            total = own + r[h][source].astype(jnp.float32) + r[h][2 + source].astype(jnp.float32)
            total = (total + far).astype(jnp.bfloat16)
            at = pl.ds((HEADS * source + h) * WIDTH, WIDTH)
            dk_out[:, at] = total[:, :WIDTH]
            dv_out[:, at] = total[:, WIDTH:]

    def send_outputs(h):
        away(od.at[:, peer_rows, head_lanes(h)], od_far.at[:, :, head_lanes(h)], o_send,
             o_recv, peer)

    for i, (src, dst) in enumerate(((k_hbm, k_in), (v_hbm, v_in))):
        near(src, dst, kv_in.at[i])
    for i, src in enumerate((q_hbm, g_hbm)):
        near(src.at[:, theirs], qg_in.at[i], qg_in_sem)
        near(src.at[:, mine], qg.at[i, token_rows], qg_own)

    zeros = jnp.zeros((BLOCK, 2 * WIDTH), jnp.float32)
    for t in range(CHIP_BLOCKS):
        parts[t, 0] = zeros
        parts[t, REACH + 1] = zeros
    base = chip * CHIP_BLOCKS
    begins, counts = [base + t for t in range(CHIP_BLOCKS)], [1] * CHIP_BLOCKS
    end = jnp.int32(0)
    for i in range(lengths.shape[0]):
        begin, end = end, end + lengths[i]
        for t in range(CHIP_BLOCKS):
            inside = (begin <= base + t) & (base + t < end)
            shown = jnp.where(fulls[i] > 0, end - begin, base + t - begin + 1)
            begins[t] = jnp.where(inside, begin, begins[t])
            counts[t] = jnp.where(inside, shown, counts[t])
    for t in range(CHIP_BLOCKS):
        first[t] = jnp.clip(begins[t] - base + OWN, t, t + OWN)
        seen[t] = counts[t]

    for kind, held in enumerate((k_in, v_in)):
        wait(held, kv_in.at[kind])
        for head in range(2 * HEADS):
            staged[head, kind] = held[:, :, pl.ds(head * WIDTH, WIDTH)]
    pl.semaphore_wait(barrier, 8)
    send_kv(0)
    wait(qg_in, qg_in_sem)
    send_queries(0)
    send_kv(1)
    send_queries(1)
    for h in range(HEADS):
        for kind in (0, 1):
            kv[h][kind, own_blocks] = staged[HEADS * core + h, kind]
    wait(qg_in, qg_own)

    for h in range(HEADS):
        wait_inputs(h)
        tiles(h)
        send_partials(h)
        send_outputs(h)
    for i, dst in enumerate((o_hbm, dq_hbm)):
        near(od.at[i, token_rows], dst.at[:, mine], o_own)
    collect(0)
    wait(od_far, o_recv)
    for i, dst in enumerate((o_hbm, dq_hbm)):
        near(od_far.at[i], dst.at[:, theirs], o_far)
    collect(1)

    for h in range(HEADS):
        wait(kv[h].at[:, : WINDOW - 2], kv_send.at[h])
        wait(r[h], r_send.at[h])
    wait(qg_in, qg_send)
    wait(od_far, o_send)
    wait(od_far, o_own)
    wait(od_far, o_far)


def settle(*refs):
    refs, (loaded, stored) = refs[:-2], refs[-2:]
    count = len(refs) // 3
    steps = []
    for i in range(count):
        src, dst, held = refs[i], refs[count + i], refs[2 * count + i]
        pieces = PIECES if held.shape == refs[0].shape else 1
        size = held.shape[0] // pieces
        for piece in range(pieces):
            at = pl.ds(piece * size, size)
            load = pltpu.make_async_copy(src.at[at], held.at[at], loaded.at[i, piece])
            store = pltpu.make_async_copy(held.at[at], dst.at[at], stored.at[i, piece])
            load.start()
            steps.append((load, store))
    for load, store in steps:
        load.wait()
        store.start()
    for load, store in steps:
        store.wait()


def per_device(queries, key_vectors, value_matrix, out_grad, clip_lengths, clip_full):
    local, wide = queries.shape
    narrow = key_vectors.shape[1]
    half = wide // 2
    low = jnp.bfloat16
    whole = pl.BlockSpec(memory_space=pltpu.HBM)
    scalars = pl.BlockSpec(memory_space=pltpu.SMEM)
    near = pl.BlockSpec(memory_space=pltpu.VMEM)
    dma = pltpu.SemaphoreType.DMA

    def some(count, shape, dtype=low):
        return [pltpu.VMEM(shape, dtype)] * count

    shapes = [jax.ShapeDtypeStruct((local, n), low) for n in (wide, wide, narrow, narrow)]
    results = pl.pallas_call(
        kernel,
        out_shape=shapes,
        in_specs=[whole] * 4 + [scalars] * 2,
        out_specs=(whole, whole, near, near),
        scratch_shapes=[
            *some(2, (local // BLOCK, BLOCK, narrow)),
            pltpu.VMEM((2 * HEADS, 2, local // BLOCK, BLOCK, WIDTH), low),
            pltpu.VMEM((2, local, half), low),
            pltpu.VMEM((2, 2 * local, half), low),
            *some(HEADS, (2, WINDOW, BLOCK, WIDTH)),
            pltpu.VMEM((2, 2 * local, half), low),
            pltpu.VMEM((2, local, half), low),
            pltpu.VMEM((CHIP_BLOCKS, REACH + 2, BLOCK, 2 * WIDTH), jnp.float32),
            *some(HEADS, (WINDOW * BLOCK, 2 * WIDTH)),
            *some(HEADS, (6, local, 2 * WIDTH)),
            pltpu.SMEM((CHIP_BLOCKS,), jnp.int32),
            pltpu.SMEM((CHIP_BLOCKS,), jnp.int32),
            dma((2,)), dma, dma, dma((HEADS,)), dma((HEADS,)), dma, dma((HEADS,)),
            dma((HEADS,)), dma((HEADS,)), dma, dma, dma, dma,
        ],
        compiler_params=pltpu.CompilerParams(
            collective_id=0, has_side_effects=True, vmem_limit_bytes=56 * 2**20
        ),
        cost_estimate=pl.CostEstimate(
            flops=12 * local * wide * SPAN,
            bytes_accessed=8 * local * (wide + narrow),
            transcendentals=local * wide // WIDTH * SPAN,
        ),
    )(
        queries,
        key_vectors.reshape(-1, BLOCK, narrow),
        value_matrix.reshape(-1, BLOCK, narrow),
        out_grad,
        clip_lengths,
        clip_full,
    )
    return pl.pallas_call(
        settle,
        out_shape=shapes,
        in_specs=[pl.BlockSpec(memory_space=pl.ANY)] * 4,
        out_specs=[whole] * 4,
        scratch_shapes=[
            *some(2, (local, wide)),
            *some(2, (local, narrow)),
            dma((4, PIECES)),
            dma((4, PIECES)),
        ],
        compiler_params=pltpu.CompilerParams(vmem_limit_bytes=56 * 2**20),
    )(*results)


def solution(mesh):
    sharded = P(("dp", "ctx"), None)
    return jax.shard_map(
        per_device,
        mesh=mesh,
        in_specs=(sharded, sharded, sharded, sharded, P("dp"), P("dp")),
        out_specs=(sharded, sharded, sharded, sharded),
        check_vma=False,
    )
```

```python
import jax
import jax.numpy as jnp
from jax import lax
from jax.experimental import pallas as pl
from jax.experimental.pallas import tpu as pltpu
from jax.sharding import PartitionSpec as P

MESH = pl.DeviceIdType.MESH
WIDTH = 128
BLOCK = 64
REACH = 6
CHIP_BLOCKS = 4
WINDOW = CHIP_BLOCKS + 2 * (REACH - 1)
OWN = REACH - 1
LEFT = OWN - CHIP_BLOCKS
RIGHT = OWN + CHIP_BLOCKS
HEADS = 2
SPAN = REACH * BLOCK
PIECES = 2
ORDER = (0, 3, 1, 2)
LOG2E = 1.4426950408889634


def kernel(
    q_hbm, k_hbm, v_hbm, g_hbm, lengths, fulls,
    o_hbm, dq_hbm, dk_out, dv_out,
    k_in, v_in, staged, qg_in, qg, kv0, kv1, od, od_far, parts, low_held, dlow_held, s0, s1, r0, r1,
    first, seen,
    kv_in, qg_in_sem, qg_own, kv_send, kv_recv, qg_send, qg_recv,
    r_send, r_recv, o_own, o_send, o_recv, o_far,
):
    kv, s, r = (kv0, kv1), (s0, s1), (r0, r1)
    rows = 2 * BLOCK
    wide = qg.shape[2]
    cols = wide // HEADS
    group = cols // WIDTH
    me, row = lax.axis_index("ctx"), lax.axis_index("dp")
    chips = lax.axis_size("ctx") // 2
    chip, core = me // 2, lax.rem(me, 2)
    other = 1 - core
    after, after2 = (lax.rem(chip + n, chips) for n in (1, 2))
    before, before2 = (lax.rem(chip + chips - n, chips) for n in (1, 2))
    peer = 2 * chip + other

    def away(src, dst, send, recv, target):
        pltpu.make_async_remote_copy(
            src_ref=src, dst_ref=dst, send_sem=send, recv_sem=recv,
            device_id=(target, row), device_id_type=MESH,
        ).start()

    def near(src, dst, sem):
        pltpu.make_async_copy(src, dst, sem).start()

    def wait(ref, sem):
        pltpu.make_async_copy(ref, ref, sem).wait()

    two_off = jnp.where(core == 0, before2, after2)
    barrier = pltpu.get_barrier_semaphore()
    for device in (
        peer, 2 * before, 2 * before + 1, 2 * after, 2 * after + 1,
        2 * two_off, 2 * two_off + 1, jnp.where(core == 0, 2 * after2, 2 * before2 + 1),
    ):
        pl.semaphore_signal(barrier, inc=1, device_id=(device, row), device_id_type=MESH)

    own_blocks = pl.ds(OWN + 2 * core, 2)
    in_after = pl.ds(LEFT + 2 * core, 2)
    in_before = pl.ds(RIGHT + 2 * core, 2)
    token_rows = pl.ds(pl.multiple_of(core * rows, rows), rows)
    peer_rows = pl.ds(pl.multiple_of(other * rows, rows), rows)
    own_rows = pl.ds(pl.multiple_of((OWN + 2 * core) * BLOCK, BLOCK), rows)
    their_rows = pl.ds(pl.multiple_of((OWN + 2 * other) * BLOCK, BLOCK), rows)
    mine = pl.ds(pl.multiple_of(core * wide, WIDTH), wide)
    theirs = pl.ds(pl.multiple_of(other * wide, WIDTH), wide)

    def head_lanes(h):
        return pl.ds(h * cols, cols)

    def send_kv(h):
        for target in (0, 1):
            src = staged.at[HEADS * target + h]
            away(src.at[:, core], kv[h].at[:, (WINDOW - 1) * other], kv_send.at[h],
                 kv_recv.at[h], 2 * two_off + target)
            away(src, kv[h].at[:, in_after], kv_send.at[h], kv_recv.at[h], 2 * after + target)
            away(src, kv[h].at[:, in_before], kv_send.at[h], kv_recv.at[h], 2 * before + target)
        away(staged.at[HEADS * other + h], kv[h].at[:, own_blocks], kv_send.at[h],
             kv_recv.at[h], peer)

    def send_queries(h):
        away(qg_in.at[:, :, head_lanes(h)], qg.at[:, token_rows, head_lanes(h)],
             qg_send, qg_recv.at[h], peer)

    def wait_inputs(h):
        wait(qg.at[:, :rows, head_lanes(h)], qg_recv.at[h])
        wait(kv[h].at[:, : WINDOW - 2], kv_recv.at[h])

    score_scale = WIDTH**-0.5
    across = (((1,), (1,)), ((), ()))
    down = (((0,), (0,)), ((), ()))

    def load(h, t):
        begin = first[t]
        tokens = pl.ds(t * BLOCK, BLOCK)

        def windowed(kind):
            return jnp.concatenate([kv[h][kind, begin + b] for b in range(REACH)], axis=0)

        def stacked(kind):
            return jnp.concatenate(
                [qg[kind, tokens, pl.ds(h * cols + m * WIDTH, WIDTH)] for m in range(group)],
                axis=0,
            )

        return windowed(0), windowed(1), stacked(0), stacked(1)

    def products(h, t):
        keys, values, query, grad = load(h, t)
        scores = lax.dot_general(keys, query, across, preferred_element_type=jnp.float32)
        dprobs = lax.dot_general(values, grad, across, preferred_element_type=jnp.float32)
        return scores, dprobs

    def softmax(t, scores, dprobs):
        count = seen[t]
        bias = [jnp.where(b < count, 0.0, -jnp.inf).astype(jnp.float32) for b in range(REACH)]
        lows, dlows = [], []
        for c in range(scores.shape[1] // WIDTH):
            lanes = slice(c * WIDTH, (c + 1) * WIDTH)
            logits = scores[:, lanes] * (score_scale * LOG2E)
            logits = jnp.concatenate(
                [logits[:BLOCK]]
                + [logits[b * BLOCK : (b + 1) * BLOCK] + bias[b] for b in range(1, REACH)],
                axis=0,
            )
            weight = jnp.exp2(logits - jnp.max(logits, axis=0, keepdims=True))
            probs = weight * (1.0 / jnp.sum(weight, axis=0, keepdims=True))
            lows.append(probs.astype(jnp.bfloat16))
            dprob = dprobs[:, lanes]
            delta = jnp.sum(probs * dprob, axis=0, keepdims=True)
            dlows.append((probs * (dprob - delta)).astype(jnp.bfloat16))
        return jnp.concatenate(lows, axis=1), jnp.concatenate(dlows, axis=1)

    def finish(h, t, low, dscores):
        _, _, query, grad = load(h, t)
        low_held[t] = low
        dlow_held[t] = dscores
        dkeys = jnp.dot(dscores, query, preferred_element_type=jnp.float32)
        dvalues = jnp.dot(low, grad, preferred_element_type=jnp.float32)
        for b in range(REACH):
            at = slice(b * BLOCK, (b + 1) * BLOCK)
            parts[t, b + 1, :, :WIDTH] = dkeys[at]
            parts[t, b + 1, :, WIDTH:] = dvalues[at]

    def tiles(h):
        made = products(h, ORDER[0])
        for i, t in enumerate(ORDER):
            ready = made
            if i + 1 < CHIP_BLOCKS:
                made = products(h, ORDER[i + 1])
            finish(h, t, *softmax(t, *ready))
            if t == 0:
                put_sums(h, 0)
                part(h, 0, 1, far_slot(h), 2 * before2 + 1)
            if t == CHIP_BLOCKS - 1:
                put_sums(h, WINDOW - 1)
                part(h, WINDOW - 1, 1, far_slot(h), 2 * after2)

    def outputs(h):
        for t in range(CHIP_BLOCKS):
            keys, values, _, _ = load(h, t)
            attn = lax.dot_general(values, low_held[t], down, preferred_element_type=jnp.float32)
            dquery = lax.dot_general(keys, dlow_held[t], down, preferred_element_type=jnp.float32)
            attn = attn.astype(jnp.bfloat16).T
            dquery = (dquery * score_scale).astype(jnp.bfloat16).T
            for m in range(group):
                at = pl.ds(h * cols + m * WIDTH, WIDTH)
                tokens = pl.ds(t * BLOCK, BLOCK)
                od[0, tokens, at] = attn[m * BLOCK : (m + 1) * BLOCK]
                od[1, tokens, at] = dquery[m * BLOCK : (m + 1) * BLOCK]

    scale_row = jnp.where(
        lax.broadcasted_iota(jnp.int32, (1, 2 * WIDTH), 1) < WIDTH, score_scale, 1.0
    ).astype(jnp.float32)

    def put_sums(h, *windows):
        for w in windows:
            total = None
            for t in range(max(0, w - 2 * OWN), min(CHIP_BLOCKS, w + 1)):
                term = parts[t, jnp.clip(w - first[t] + 1, 0, REACH + 1)]
                total = term if total is None else total + term
            s[h][pl.ds(w * BLOCK, BLOCK), :] = (total * scale_row).astype(jnp.bfloat16)

    def part(h, w, count, slot, target):
        away(s[h].at[pl.ds(w * BLOCK, count * BLOCK)], slot, r_send.at[h], r_recv.at[h], target)

    def far_slot(h):
        return r[h].at[5, pl.ds(pl.multiple_of(core * BLOCK, BLOCK), BLOCK)]

    def send_partials(h):
        put_sums(h, 1, 2, 9, 10)
        part(h, LEFT, 2, r[h].at[2 + core], 2 * before)
        part(h, RIGHT, 2, r[h].at[core], 2 * after)
        put_sums(h, 3, 4, 11, 12)
        part(h, LEFT + 2, 2, r[h].at[2 + core], 2 * before + 1)
        part(h, RIGHT + 2, 2, r[h].at[core], 2 * after + 1)
        put_sums(h, *range(OWN, RIGHT))
        away(s[h].at[their_rows], r[h].at[4], r_send.at[h], r_recv.at[h], peer)

    def collect(h):
        wait(r[h], r_recv.at[h])
        nothing = jnp.zeros((BLOCK, 2 * WIDTH), jnp.float32)
        for source in (0, 1):
            own = jnp.where(core == source, s[h][own_rows, :].astype(jnp.float32),
                            r[h][4].astype(jnp.float32))
            far = r[h][5, pl.ds(source * BLOCK, BLOCK)].astype(jnp.float32)
            far = jnp.concatenate(
                [jnp.where(core == 0, far, nothing), jnp.where(core == 1, far, nothing)], axis=0
            )
            total = own + r[h][source].astype(jnp.float32) + r[h][2 + source].astype(jnp.float32)
            total = (total + far).astype(jnp.bfloat16)
            at = pl.ds((HEADS * source + h) * WIDTH, WIDTH)
            dk_out[:, at] = total[:, :WIDTH]
            dv_out[:, at] = total[:, WIDTH:]

    def send_outputs(h):
        away(od.at[:, peer_rows, head_lanes(h)], od_far.at[:, :, head_lanes(h)], o_send,
             o_recv, peer)

    for i, (src, dst) in enumerate(((k_hbm, k_in), (v_hbm, v_in))):
        near(src, dst, kv_in.at[i])
    for i, src in enumerate((q_hbm, g_hbm)):
        near(src.at[:, theirs], qg_in.at[i], qg_in_sem)
        near(src.at[:, mine], qg.at[i, token_rows], qg_own)

    zeros = jnp.zeros((BLOCK, 2 * WIDTH), jnp.float32)
    for t in range(CHIP_BLOCKS):
        parts[t, 0] = zeros
        parts[t, REACH + 1] = zeros
    base = chip * CHIP_BLOCKS
    begins, counts = [base + t for t in range(CHIP_BLOCKS)], [1] * CHIP_BLOCKS
    end = jnp.int32(0)
    for i in range(lengths.shape[0]):
        begin, end = end, end + lengths[i]
        for t in range(CHIP_BLOCKS):
            inside = (begin <= base + t) & (base + t < end)
            shown = jnp.where(fulls[i] > 0, end - begin, base + t - begin + 1)
            begins[t] = jnp.where(inside, begin, begins[t])
            counts[t] = jnp.where(inside, shown, counts[t])
    for t in range(CHIP_BLOCKS):
        first[t] = jnp.clip(begins[t] - base + OWN, t, t + OWN)
        seen[t] = counts[t]

    for kind, held in enumerate((k_in, v_in)):
        wait(held, kv_in.at[kind])
        for head in range(2 * HEADS):
            staged[head, kind] = held[:, :, pl.ds(head * WIDTH, WIDTH)]
    pl.semaphore_wait(barrier, 8)
    send_kv(0)
    wait(qg_in, qg_in_sem)
    send_queries(0)
    for h in range(HEADS):
        for kind in (0, 1):
            kv[h][kind, own_blocks] = staged[HEADS * core + h, kind]
    wait(qg_in, qg_own)
    for h in range(1, HEADS):
        wait(kv[h - 1].at[:, : WINDOW - 2], kv_send.at[h - 1])
        send_kv(h)
        send_queries(h)

    for h in range(HEADS):
        wait_inputs(h)
        tiles(h)
        send_partials(h)
        outputs(h)
        send_outputs(h)
    for i, dst in enumerate((o_hbm, dq_hbm)):
        near(od.at[i, token_rows], dst.at[:, mine], o_own)
    collect(0)
    wait(od_far, o_recv)
    for i, dst in enumerate((o_hbm, dq_hbm)):
        near(od_far.at[i], dst.at[:, theirs], o_far)
    collect(1)

    wait(kv[HEADS - 1].at[:, : WINDOW - 2], kv_send.at[HEADS - 1])
    for h in range(HEADS):
        wait(r[h], r_send.at[h])
    wait(qg_in, qg_send)
    wait(od_far, o_send)
    wait(od_far, o_own)
    wait(od_far, o_far)


def settle(*refs):
    refs, (loaded, stored) = refs[:-2], refs[-2:]
    count = len(refs) // 3
    steps = []
    for i in range(count):
        src, dst, held = refs[i], refs[count + i], refs[2 * count + i]
        pieces = PIECES if held.shape == refs[0].shape else 1
        size = held.shape[0] // pieces
        for piece in range(pieces):
            at = pl.ds(piece * size, size)
            load = pltpu.make_async_copy(src.at[at], held.at[at], loaded.at[i, piece])
            store = pltpu.make_async_copy(held.at[at], dst.at[at], stored.at[i, piece])
            load.start()
            steps.append((load, store))
    for load, store in steps:
        load.wait()
        store.start()
    for load, store in steps:
        store.wait()


def per_device(queries, key_vectors, value_matrix, out_grad, clip_lengths, clip_full):
    local, wide = queries.shape
    narrow = key_vectors.shape[1]
    half = wide // 2
    low = jnp.bfloat16
    whole = pl.BlockSpec(memory_space=pltpu.HBM)
    scalars = pl.BlockSpec(memory_space=pltpu.SMEM)
    near = pl.BlockSpec(memory_space=pltpu.VMEM)
    dma = pltpu.SemaphoreType.DMA

    def some(count, shape, dtype=low):
        return [pltpu.VMEM(shape, dtype)] * count

    shapes = [jax.ShapeDtypeStruct((local, n), low) for n in (wide, wide, narrow, narrow)]
    results = pl.pallas_call(
        kernel,
        out_shape=shapes,
        in_specs=[whole] * 4 + [scalars] * 2,
        out_specs=(whole, whole, near, near),
        scratch_shapes=[
            *some(2, (local // BLOCK, BLOCK, narrow)),
            pltpu.VMEM((2 * HEADS, 2, local // BLOCK, BLOCK, WIDTH), low),
            pltpu.VMEM((2, local, half), low),
            pltpu.VMEM((2, 2 * local, half), low),
            *some(HEADS, (2, WINDOW, BLOCK, WIDTH)),
            pltpu.VMEM((2, 2 * local, half), low),
            pltpu.VMEM((2, local, half), low),
            pltpu.VMEM((CHIP_BLOCKS, REACH + 2, BLOCK, 2 * WIDTH), jnp.float32),
            *some(2, (CHIP_BLOCKS, SPAN, half // HEADS // WIDTH * BLOCK)),
            *some(HEADS, (WINDOW * BLOCK, 2 * WIDTH)),
            *some(HEADS, (6, local, 2 * WIDTH)),
            pltpu.SMEM((CHIP_BLOCKS,), jnp.int32),
            pltpu.SMEM((CHIP_BLOCKS,), jnp.int32),
            dma((2,)), dma, dma, dma((HEADS,)), dma((HEADS,)), dma, dma((HEADS,)),
            dma((HEADS,)), dma((HEADS,)), dma, dma, dma, dma,
        ],
        compiler_params=pltpu.CompilerParams(
            collective_id=0, has_side_effects=True, vmem_limit_bytes=56 * 2**20
        ),
        cost_estimate=pl.CostEstimate(
            flops=12 * local * wide * SPAN,
            bytes_accessed=8 * local * (wide + narrow),
            transcendentals=local * wide // WIDTH * SPAN,
        ),
    )(
        queries,
        key_vectors.reshape(-1, BLOCK, narrow),
        value_matrix.reshape(-1, BLOCK, narrow),
        out_grad,
        clip_lengths,
        clip_full,
    )
    return pl.pallas_call(
        settle,
        out_shape=shapes,
        in_specs=[pl.BlockSpec(memory_space=pl.ANY)] * 4,
        out_specs=[whole] * 4,
        scratch_shapes=[
            *some(2, (local, wide)),
            *some(2, (local, narrow)),
            dma((4, PIECES)),
            dma((4, PIECES)),
        ],
        compiler_params=pltpu.CompilerParams(vmem_limit_bytes=56 * 2**20),
    )(*results)


def solution(mesh):
    sharded = P(("dp", "ctx"), None)
    return jax.shard_map(
        per_device,
        mesh=mesh,
        in_specs=(sharded, sharded, sharded, sharded, P("dp"), P("dp")),
        out_specs=(sharded, sharded, sharded, sharded),
        check_vma=False,
    )
```

```python
import jax
import jax.numpy as jnp
from jax import lax
from jax.experimental import pallas as pl
from jax.experimental.pallas import tpu as pltpu
from jax.sharding import PartitionSpec as P

MESH = pl.DeviceIdType.MESH
WIDTH = 128
BLOCK = 64
REACH = 6
CHIP_BLOCKS = 4
WINDOW = CHIP_BLOCKS + 2 * (REACH - 1)
OWN = REACH - 1
LEFT = OWN - CHIP_BLOCKS
RIGHT = OWN + CHIP_BLOCKS
HEADS = 2
SPAN = REACH * BLOCK
PIECES = 2
ORDER = (0, 3, 1, 2)
LOG2E = 1.4426950408889634


def kernel(
    q_hbm, k_hbm, v_hbm, g_hbm, lengths, fulls,
    o_hbm, dq_hbm, dk_out, dv_out,
    k_in, v_in, staged, qg_in, qg, kv0, kv1, od, od_far, parts, low_held, dlow_held, s0, s1, x0, x1, r0, r1,
    first, seen,
    kv_in, qg_in_sem, qg_own, kv_send, kv_recv, qg_send, qg_recv,
    x_send, x_recv, r_send, r_recv, o_own, o_send, o_recv, o_far,
):
    kv, s, x, r = (kv0, kv1), (s0, s1), (x0, x1), (r0, r1)
    rows = 2 * BLOCK
    wide = qg.shape[2]
    cols = wide // HEADS
    group = cols // WIDTH
    me, row = lax.axis_index("ctx"), lax.axis_index("dp")
    chips = lax.axis_size("ctx") // 2
    chip, core = me // 2, lax.rem(me, 2)
    other = 1 - core
    after, after2 = (lax.rem(chip + n, chips) for n in (1, 2))
    before, before2 = (lax.rem(chip + chips - n, chips) for n in (1, 2))
    peer = 2 * chip + other

    def away(src, dst, send, recv, target):
        pltpu.make_async_remote_copy(
            src_ref=src, dst_ref=dst, send_sem=send, recv_sem=recv,
            device_id=(target, row), device_id_type=MESH,
        ).start()

    def near(src, dst, sem):
        pltpu.make_async_copy(src, dst, sem).start()

    def wait(ref, sem):
        pltpu.make_async_copy(ref, ref, sem).wait()

    two_off = jnp.where(core == 0, before2, after2)
    barrier = pltpu.get_barrier_semaphore()
    for device in (
        peer, 2 * before, 2 * before + 1, 2 * after, 2 * after + 1,
        2 * two_off, 2 * two_off + 1, jnp.where(core == 0, 2 * after2, 2 * before2 + 1),
    ):
        pl.semaphore_signal(barrier, inc=1, device_id=(device, row), device_id_type=MESH)

    own_blocks = pl.ds(OWN + 2 * core, 2)
    in_after = pl.ds(LEFT + 2 * core, 2)
    in_before = pl.ds(RIGHT + 2 * core, 2)
    token_rows = pl.ds(pl.multiple_of(core * rows, rows), rows)
    peer_rows = pl.ds(pl.multiple_of(other * rows, rows), rows)
    own_rows = pl.ds(pl.multiple_of((OWN + 2 * core) * BLOCK, BLOCK), rows)
    their_rows = pl.ds(pl.multiple_of((OWN + 2 * other) * BLOCK, BLOCK), rows)
    mine = pl.ds(pl.multiple_of(core * wide, WIDTH), wide)
    theirs = pl.ds(pl.multiple_of(other * wide, WIDTH), wide)

    def head_lanes(h):
        return pl.ds(h * cols, cols)

    def send_kv(h):
        for target in (0, 1):
            src = staged.at[HEADS * target + h]
            away(src.at[:, core], kv[h].at[:, (WINDOW - 1) * other], kv_send.at[h],
                 kv_recv.at[h], 2 * two_off + target)
            away(src, kv[h].at[:, in_after], kv_send.at[h], kv_recv.at[h], 2 * after + target)
            away(src, kv[h].at[:, in_before], kv_send.at[h], kv_recv.at[h], 2 * before + target)
        away(staged.at[HEADS * other + h], kv[h].at[:, own_blocks], kv_send.at[h],
             kv_recv.at[h], peer)

    def send_queries(h):
        away(qg_in.at[:, :, head_lanes(h)], qg.at[:, token_rows, head_lanes(h)],
             qg_send, qg_recv.at[h], peer)

    def wait_inputs(h):
        wait(qg.at[:, :rows, head_lanes(h)], qg_recv.at[h])
        wait(kv[h].at[:, : WINDOW - 2], kv_recv.at[h])

    score_scale = WIDTH**-0.5
    across = (((1,), (1,)), ((), ()))
    down = (((0,), (0,)), ((), ()))

    def load(h, t):
        begin = first[t]
        tokens = pl.ds(t * BLOCK, BLOCK)

        def windowed(kind):
            return jnp.concatenate([kv[h][kind, begin + b] for b in range(REACH)], axis=0)

        def stacked(kind):
            return jnp.concatenate(
                [qg[kind, tokens, pl.ds(h * cols + m * WIDTH, WIDTH)] for m in range(group)],
                axis=0,
            )

        return windowed(0), windowed(1), stacked(0), stacked(1)

    def products(h, t):
        keys, values, query, grad = load(h, t)
        scores = lax.dot_general(keys, query, across, preferred_element_type=jnp.float32)
        dprobs = lax.dot_general(values, grad, across, preferred_element_type=jnp.float32)
        return scores, dprobs

    def softmax(t, scores, dprobs):
        count = seen[t]
        bias = [jnp.where(b < count, 0.0, -jnp.inf).astype(jnp.float32) for b in range(REACH)]
        lows, dlows = [], []
        for c in range(scores.shape[1] // WIDTH):
            lanes = slice(c * WIDTH, (c + 1) * WIDTH)
            logits = scores[:, lanes] * (score_scale * LOG2E)
            logits = jnp.concatenate(
                [logits[:BLOCK]]
                + [logits[b * BLOCK : (b + 1) * BLOCK] + bias[b] for b in range(1, REACH)],
                axis=0,
            )
            weight = jnp.exp2(logits - jnp.max(logits, axis=0, keepdims=True))
            probs = weight * (1.0 / jnp.sum(weight, axis=0, keepdims=True))
            lows.append(probs.astype(jnp.bfloat16))
            dprob = dprobs[:, lanes]
            delta = jnp.sum(probs * dprob, axis=0, keepdims=True)
            dlows.append((probs * (dprob - delta)).astype(jnp.bfloat16))
        return jnp.concatenate(lows, axis=1), jnp.concatenate(dlows, axis=1)

    def finish(h, t, low, dscores):
        _, _, query, grad = load(h, t)
        low_held[t] = low
        dlow_held[t] = dscores
        dkeys = jnp.dot(dscores, query, preferred_element_type=jnp.float32)
        dvalues = jnp.dot(low, grad, preferred_element_type=jnp.float32)
        for b in range(REACH):
            at = slice(b * BLOCK, (b + 1) * BLOCK)
            parts[t, b + 1, :, :WIDTH] = dkeys[at]
            parts[t, b + 1, :, WIDTH:] = dvalues[at]

    def tiles(h):
        made = products(h, ORDER[0])
        for i, t in enumerate(ORDER):
            ready = made
            if i + 1 < CHIP_BLOCKS:
                made = products(h, ORDER[i + 1])
            finish(h, t, *softmax(t, *ready))
            if t == 0:
                put_sums(h, 0)
                away(s[h].at[pl.ds(0, BLOCK)], x[h].at[1], x_send.at[h], x_recv.at[h, 1],
                     2 * before + core)
            if t == CHIP_BLOCKS - 1:
                put_sums(h, WINDOW - 1)
                away(s[h].at[pl.ds((WINDOW - 1) * BLOCK, BLOCK)], x[h].at[0], x_send.at[h],
                     x_recv.at[h, 0], 2 * after + core)

    def outputs(h):
        for t in range(CHIP_BLOCKS):
            keys, values, _, _ = load(h, t)
            attn = lax.dot_general(values, low_held[t], down, preferred_element_type=jnp.float32)
            dquery = lax.dot_general(keys, dlow_held[t], down, preferred_element_type=jnp.float32)
            attn = attn.astype(jnp.bfloat16).T
            dquery = (dquery * score_scale).astype(jnp.bfloat16).T
            for m in range(group):
                at = pl.ds(h * cols + m * WIDTH, WIDTH)
                tokens = pl.ds(t * BLOCK, BLOCK)
                od[0, tokens, at] = attn[m * BLOCK : (m + 1) * BLOCK]
                od[1, tokens, at] = dquery[m * BLOCK : (m + 1) * BLOCK]

    scale_row = jnp.where(
        lax.broadcasted_iota(jnp.int32, (1, 2 * WIDTH), 1) < WIDTH, score_scale, 1.0
    ).astype(jnp.float32)

    def put_sums(h, *windows, more=None):
        for w in windows:
            total = None
            for t in range(max(0, w - 2 * OWN), min(CHIP_BLOCKS, w + 1)):
                term = parts[t, jnp.clip(w - first[t] + 1, 0, REACH + 1)]
                total = term if total is None else total + term
            total = total * scale_row
            if more is not None:
                total = total + more.astype(jnp.float32)
            s[h][pl.ds(w * BLOCK, BLOCK), :] = total.astype(jnp.bfloat16)

    def part(h, w, slot, target):
        away(s[h].at[pl.ds(w * BLOCK, 2 * BLOCK)], slot, r_send.at[h], r_recv.at[h], target)

    def send_partials(h):
        put_sums(h, 1, 2, 11, 12)
        part(h, LEFT, r[h].at[2 + core], 2 * before)
        part(h, RIGHT + 2, r[h].at[core], 2 * after + 1)
        put_sums(h, *range(OWN, RIGHT))
        away(s[h].at[their_rows], r[h].at[4], r_send.at[h], r_recv.at[h], peer)
        put_sums(h, 3, 10)

    def send_edges(h):
        wait(x[h].at[1], x_recv.at[h, 1])
        put_sums(h, OWN - 1, more=x[h][1])
        part(h, LEFT + 2, r[h].at[2 + core], 2 * before + 1)
        wait(x[h].at[0], x_recv.at[h, 0])
        put_sums(h, RIGHT, more=x[h][0])
        part(h, RIGHT, r[h].at[core], 2 * after)

    def collect(h):
        wait(r[h], r_recv.at[h])
        for source in (0, 1):
            own = jnp.where(core == source, s[h][own_rows, :].astype(jnp.float32),
                            r[h][4].astype(jnp.float32))
            total = own + r[h][source].astype(jnp.float32) + r[h][2 + source].astype(jnp.float32)
            total = total.astype(jnp.bfloat16)
            at = pl.ds((HEADS * source + h) * WIDTH, WIDTH)
            dk_out[:, at] = total[:, :WIDTH]
            dv_out[:, at] = total[:, WIDTH:]

    def send_outputs(h):
        away(od.at[:, peer_rows, head_lanes(h)], od_far.at[:, :, head_lanes(h)], o_send,
             o_recv, peer)

    for i, (src, dst) in enumerate(((k_hbm, k_in), (v_hbm, v_in))):
        near(src, dst, kv_in.at[i])
    for i, src in enumerate((q_hbm, g_hbm)):
        near(src.at[:, theirs], qg_in.at[i], qg_in_sem)
        near(src.at[:, mine], qg.at[i, token_rows], qg_own)

    zeros = jnp.zeros((BLOCK, 2 * WIDTH), jnp.float32)
    for t in range(CHIP_BLOCKS):
        parts[t, 0] = zeros
        parts[t, REACH + 1] = zeros
    base = chip * CHIP_BLOCKS
    begins, counts = [base + t for t in range(CHIP_BLOCKS)], [1] * CHIP_BLOCKS
    end = jnp.int32(0)
    for i in range(lengths.shape[0]):
        begin, end = end, end + lengths[i]
        for t in range(CHIP_BLOCKS):
            inside = (begin <= base + t) & (base + t < end)
            shown = jnp.where(fulls[i] > 0, end - begin, base + t - begin + 1)
            begins[t] = jnp.where(inside, begin, begins[t])
            counts[t] = jnp.where(inside, shown, counts[t])
    for t in range(CHIP_BLOCKS):
        first[t] = jnp.clip(begins[t] - base + OWN, t, t + OWN)
        seen[t] = counts[t]

    for kind, held in enumerate((k_in, v_in)):
        wait(held, kv_in.at[kind])
        for head in range(2 * HEADS):
            staged[head, kind] = held[:, :, pl.ds(head * WIDTH, WIDTH)]
    pl.semaphore_wait(barrier, 8)
    send_kv(0)
    wait(qg_in, qg_in_sem)
    send_queries(0)
    for h in range(HEADS):
        for kind in (0, 1):
            kv[h][kind, own_blocks] = staged[HEADS * core + h, kind]
    wait(qg_in, qg_own)
    for h in range(1, HEADS):
        wait(kv[h - 1].at[:, : WINDOW - 2], kv_send.at[h - 1])
        send_kv(h)
        send_queries(h)

    for h in range(HEADS):
        wait_inputs(h)
        tiles(h)
        send_partials(h)
        outputs(h)
        send_edges(h)
        send_outputs(h)
    for i, dst in enumerate((o_hbm, dq_hbm)):
        near(od.at[i, token_rows], dst.at[:, mine], o_own)
    collect(0)
    wait(od_far, o_recv)
    for i, dst in enumerate((o_hbm, dq_hbm)):
        near(od_far.at[i], dst.at[:, theirs], o_far)
    collect(1)

    wait(kv[HEADS - 1].at[:, : WINDOW - 2], kv_send.at[HEADS - 1])
    for h in range(HEADS):
        wait(r[h], r_send.at[h])
        wait(x[h], x_send.at[h])
    wait(qg_in, qg_send)
    wait(od_far, o_send)
    wait(od_far, o_own)
    wait(od_far, o_far)


def settle(*refs):
    refs, (loaded, stored) = refs[:-2], refs[-2:]
    count = len(refs) // 3
    steps = []
    for i in range(count):
        src, dst, held = refs[i], refs[count + i], refs[2 * count + i]
        pieces = PIECES if held.shape == refs[0].shape else 1
        size = held.shape[0] // pieces
        for piece in range(pieces):
            at = pl.ds(piece * size, size)
            load = pltpu.make_async_copy(src.at[at], held.at[at], loaded.at[i, piece])
            store = pltpu.make_async_copy(held.at[at], dst.at[at], stored.at[i, piece])
            load.start()
            steps.append((load, store))
    for load, store in steps:
        load.wait()
        store.start()
    for load, store in steps:
        store.wait()


def per_device(queries, key_vectors, value_matrix, out_grad, clip_lengths, clip_full):
    local, wide = queries.shape
    narrow = key_vectors.shape[1]
    half = wide // 2
    low = jnp.bfloat16
    whole = pl.BlockSpec(memory_space=pltpu.HBM)
    scalars = pl.BlockSpec(memory_space=pltpu.SMEM)
    near = pl.BlockSpec(memory_space=pltpu.VMEM)
    dma = pltpu.SemaphoreType.DMA

    def some(count, shape, dtype=low):
        return [pltpu.VMEM(shape, dtype)] * count

    shapes = [jax.ShapeDtypeStruct((local, n), low) for n in (wide, wide, narrow, narrow)]
    results = pl.pallas_call(
        kernel,
        out_shape=shapes,
        in_specs=[whole] * 4 + [scalars] * 2,
        out_specs=(whole, whole, near, near),
        scratch_shapes=[
            *some(2, (local // BLOCK, BLOCK, narrow)),
            pltpu.VMEM((2 * HEADS, 2, local // BLOCK, BLOCK, WIDTH), low),
            pltpu.VMEM((2, local, half), low),
            pltpu.VMEM((2, 2 * local, half), low),
            *some(HEADS, (2, WINDOW, BLOCK, WIDTH)),
            pltpu.VMEM((2, 2 * local, half), low),
            pltpu.VMEM((2, local, half), low),
            pltpu.VMEM((CHIP_BLOCKS, REACH + 2, BLOCK, 2 * WIDTH), jnp.float32),
            *some(2, (CHIP_BLOCKS, SPAN, half // HEADS // WIDTH * BLOCK)),
            *some(HEADS, (WINDOW * BLOCK, 2 * WIDTH)),
            *some(HEADS, (2, BLOCK, 2 * WIDTH)),
            *some(HEADS, (5, local, 2 * WIDTH)),
            pltpu.SMEM((CHIP_BLOCKS,), jnp.int32),
            pltpu.SMEM((CHIP_BLOCKS,), jnp.int32),
            dma((2,)), dma, dma, dma((HEADS,)), dma((HEADS,)), dma, dma((HEADS,)),
            dma((HEADS,)), dma((HEADS, 2)), dma((HEADS,)), dma((HEADS,)), dma, dma, dma, dma,
        ],
        compiler_params=pltpu.CompilerParams(
            collective_id=0, has_side_effects=True, vmem_limit_bytes=56 * 2**20
        ),
        cost_estimate=pl.CostEstimate(
            flops=12 * local * wide * SPAN,
            bytes_accessed=8 * local * (wide + narrow),
            transcendentals=local * wide // WIDTH * SPAN,
        ),
    )(
        queries,
        key_vectors.reshape(-1, BLOCK, narrow),
        value_matrix.reshape(-1, BLOCK, narrow),
        out_grad,
        clip_lengths,
        clip_full,
    )
    return pl.pallas_call(
        settle,
        out_shape=shapes,
        in_specs=[pl.BlockSpec(memory_space=pl.ANY)] * 4,
        out_specs=[whole] * 4,
        scratch_shapes=[
            *some(2, (local, wide)),
            *some(2, (local, narrow)),
            dma((4, PIECES)),
            dma((4, PIECES)),
        ],
        compiler_params=pltpu.CompilerParams(vmem_limit_bytes=56 * 2**20),
    )(*results)


def solution(mesh):
    sharded = P(("dp", "ctx"), None)
    return jax.shard_map(
        per_device,
        mesh=mesh,
        in_specs=(sharded, sharded, sharded, sharded, P("dp"), P("dp")),
        out_specs=(sharded, sharded, sharded, sharded),
        check_vma=False,
    )
```

```python
import jax
import jax.numpy as jnp
from jax import lax
from jax.experimental import pallas as pl
from jax.experimental.pallas import tpu as pltpu
from jax.sharding import PartitionSpec as P

MESH = pl.DeviceIdType.MESH
WIDTH = 128
BLOCK = 64
REACH = 6
CHIP_BLOCKS = 4
WINDOW = CHIP_BLOCKS + 2 * (REACH - 1)
OWN = REACH - 1
LEFT = OWN - CHIP_BLOCKS
RIGHT = OWN + CHIP_BLOCKS
HEADS = 2
SPAN = REACH * BLOCK
PIECES = 2
LOG2E = 1.4426950408889634


def kernel(
    q_hbm, k_hbm, v_hbm, g_hbm, lengths, fulls,
    o_hbm, dq_hbm, dk_out, dv_out,
    k_in, v_in, staged, qg_in, qg, kv0, kv1, od, od_far, parts, low_held, dlow_held, s0, s1, r0, r1,
    first, seen,
    kv_in, qg_in_sem, qg_own, kv_send, kv_recv, qg_send, qg_recv,
    r_send, r_recv, o_own, o_send, o_recv, o_far,
):
    kv, s, r = (kv0, kv1), (s0, s1), (r0, r1)
    rows = 2 * BLOCK
    wide = qg.shape[2]
    cols = wide // HEADS
    group = cols // WIDTH
    me, row = lax.axis_index("ctx"), lax.axis_index("dp")
    chips = lax.axis_size("ctx") // 2
    chip, core = me // 2, lax.rem(me, 2)
    other = 1 - core
    after, after2 = (lax.rem(chip + n, chips) for n in (1, 2))
    before, before2 = (lax.rem(chip + chips - n, chips) for n in (1, 2))
    peer = 2 * chip + other

    def away(src, dst, send, recv, target):
        pltpu.make_async_remote_copy(
            src_ref=src, dst_ref=dst, send_sem=send, recv_sem=recv,
            device_id=(target, row), device_id_type=MESH,
        ).start()

    def near(src, dst, sem):
        pltpu.make_async_copy(src, dst, sem).start()

    def wait(ref, sem):
        pltpu.make_async_copy(ref, ref, sem).wait()

    two_off = jnp.where(core == 0, before2, after2)
    barrier = pltpu.get_barrier_semaphore()
    for device in (
        peer, 2 * before, 2 * before + 1, 2 * after, 2 * after + 1,
        2 * two_off, 2 * two_off + 1, jnp.where(core == 0, 2 * after2, 2 * before2 + 1),
    ):
        pl.semaphore_signal(barrier, inc=1, device_id=(device, row), device_id_type=MESH)

    own_blocks = pl.ds(OWN + 2 * core, 2)
    in_after = pl.ds(LEFT + 2 * core, 2)
    in_before = pl.ds(RIGHT + 2 * core, 2)
    token_rows = pl.ds(pl.multiple_of(core * rows, rows), rows)
    peer_rows = pl.ds(pl.multiple_of(other * rows, rows), rows)
    own_rows = pl.ds(pl.multiple_of((OWN + 2 * core) * BLOCK, BLOCK), rows)
    their_rows = pl.ds(pl.multiple_of((OWN + 2 * other) * BLOCK, BLOCK), rows)
    mine = pl.ds(pl.multiple_of(core * wide, WIDTH), wide)
    theirs = pl.ds(pl.multiple_of(other * wide, WIDTH), wide)

    def head_lanes(h):
        return pl.ds(h * cols, cols)

    def send_kv(h):
        for target in (0, 1):
            src = staged.at[HEADS * target + h]
            away(src.at[:, core], kv[h].at[:, (WINDOW - 1) * other], kv_send.at[h],
                 kv_recv.at[h], 2 * two_off + target)
            away(src, kv[h].at[:, in_after], kv_send.at[h], kv_recv.at[h], 2 * after + target)
            away(src, kv[h].at[:, in_before], kv_send.at[h], kv_recv.at[h], 2 * before + target)
        away(staged.at[HEADS * other + h], kv[h].at[:, own_blocks], kv_send.at[h],
             kv_recv.at[h], peer)

    def send_queries(h):
        away(qg_in.at[:, :, head_lanes(h)], qg.at[:, token_rows, head_lanes(h)],
             qg_send, qg_recv.at[h], peer)

    def wait_inputs(h):
        wait(qg.at[:, :rows, head_lanes(h)], qg_recv.at[h])
        wait(kv[h].at[:, : WINDOW - 2], kv_recv.at[h])

    score_scale = WIDTH**-0.5
    across = (((1,), (1,)), ((), ()))
    down = (((0,), (0,)), ((), ()))

    def tokens_of(t):
        return pl.ds(pl.multiple_of(t * BLOCK, BLOCK), BLOCK)

    def each_block(work):
        def step(t, carry):
            work(t)
            return carry

        lax.fori_loop(0, CHIP_BLOCKS, step, 0)

    def load(h, t):
        begin = first[t]
        tokens = tokens_of(t)

        def windowed(kind):
            return jnp.concatenate([kv[h][kind, begin + b] for b in range(REACH)], axis=0)

        def stacked(kind):
            return jnp.concatenate(
                [qg[kind, tokens, pl.ds(h * cols + m * WIDTH, WIDTH)] for m in range(group)],
                axis=0,
            )

        return windowed(0), windowed(1), stacked(0), stacked(1)

    def products(h, t):
        keys, values, query, grad = load(h, t)
        scores = lax.dot_general(keys, query, across, preferred_element_type=jnp.float32)
        dprobs = lax.dot_general(values, grad, across, preferred_element_type=jnp.float32)
        return scores, dprobs

    def softmax(t, scores, dprobs):
        count = seen[t]
        bias = [jnp.where(b < count, 0.0, -jnp.inf).astype(jnp.float32) for b in range(REACH)]
        lows, dlows = [], []
        for c in range(scores.shape[1] // WIDTH):
            lanes = slice(c * WIDTH, (c + 1) * WIDTH)
            logits = scores[:, lanes] * (score_scale * LOG2E)
            logits = jnp.concatenate(
                [logits[:BLOCK]]
                + [logits[b * BLOCK : (b + 1) * BLOCK] + bias[b] for b in range(1, REACH)],
                axis=0,
            )
            weight = jnp.exp2(logits - jnp.max(logits, axis=0, keepdims=True))
            probs = weight * (1.0 / jnp.sum(weight, axis=0, keepdims=True))
            lows.append(probs.astype(jnp.bfloat16))
            dprob = dprobs[:, lanes]
            delta = jnp.sum(probs * dprob, axis=0, keepdims=True)
            dlows.append((probs * (dprob - delta)).astype(jnp.bfloat16))
        return jnp.concatenate(lows, axis=1), jnp.concatenate(dlows, axis=1)

    def finish(h, t, low, dscores):
        _, _, query, grad = load(h, t)
        low_held[t] = low
        dlow_held[t] = dscores
        dkeys = jnp.dot(dscores, query, preferred_element_type=jnp.float32)
        dvalues = jnp.dot(low, grad, preferred_element_type=jnp.float32)
        for b in range(REACH):
            at = slice(b * BLOCK, (b + 1) * BLOCK)
            parts[t, b + 1, :, :WIDTH] = dkeys[at]
            parts[t, b + 1, :, WIDTH:] = dvalues[at]

    def tiles(h):
        each_block(lambda t: finish(h, t, *softmax(t, *products(h, t))))
        put_sums(h, 0, WINDOW - 1)
        part(h, 0, 1, far_slot(h), 2 * before2 + 1)
        part(h, WINDOW - 1, 1, far_slot(h), 2 * after2)

    def outputs(h):
        def work(t):
            keys, values, _, _ = load(h, t)
            attn = lax.dot_general(values, low_held[t], down, preferred_element_type=jnp.float32)
            dquery = lax.dot_general(keys, dlow_held[t], down, preferred_element_type=jnp.float32)
            attn = attn.astype(jnp.bfloat16).T
            dquery = (dquery * score_scale).astype(jnp.bfloat16).T
            for m in range(group):
                at = pl.ds(h * cols + m * WIDTH, WIDTH)
                od[0, tokens_of(t), at] = attn[m * BLOCK : (m + 1) * BLOCK]
                od[1, tokens_of(t), at] = dquery[m * BLOCK : (m + 1) * BLOCK]

        each_block(work)

    scale_row = jnp.where(
        lax.broadcasted_iota(jnp.int32, (1, 2 * WIDTH), 1) < WIDTH, score_scale, 1.0
    ).astype(jnp.float32)

    def put_sums(h, *windows):
        for w in windows:
            total = None
            for t in range(max(0, w - 2 * OWN), min(CHIP_BLOCKS, w + 1)):
                term = parts[t, jnp.clip(w - first[t] + 1, 0, REACH + 1)]
                total = term if total is None else total + term
            s[h][pl.ds(w * BLOCK, BLOCK), :] = (total * scale_row).astype(jnp.bfloat16)

    def part(h, w, count, slot, target):
        away(s[h].at[pl.ds(w * BLOCK, count * BLOCK)], slot, r_send.at[h], r_recv.at[h], target)

    def far_slot(h):
        return r[h].at[5, pl.ds(pl.multiple_of(core * BLOCK, BLOCK), BLOCK)]

    def send_partials(h):
        put_sums(h, 1, 2, 9, 10)
        part(h, LEFT, 2, r[h].at[2 + core], 2 * before)
        part(h, RIGHT, 2, r[h].at[core], 2 * after)
        put_sums(h, 3, 4, 11, 12)
        part(h, LEFT + 2, 2, r[h].at[2 + core], 2 * before + 1)
        part(h, RIGHT + 2, 2, r[h].at[core], 2 * after + 1)
        put_sums(h, *range(OWN, RIGHT))
        away(s[h].at[their_rows], r[h].at[4], r_send.at[h], r_recv.at[h], peer)

    def collect(h):
        wait(r[h], r_recv.at[h])
        nothing = jnp.zeros((BLOCK, 2 * WIDTH), jnp.float32)
        for source in (0, 1):
            own = jnp.where(core == source, s[h][own_rows, :].astype(jnp.float32),
                            r[h][4].astype(jnp.float32))
            far = r[h][5, pl.ds(source * BLOCK, BLOCK)].astype(jnp.float32)
            far = jnp.concatenate(
                [jnp.where(core == 0, far, nothing), jnp.where(core == 1, far, nothing)], axis=0
            )
            total = own + r[h][source].astype(jnp.float32) + r[h][2 + source].astype(jnp.float32)
            total = (total + far).astype(jnp.bfloat16)
            at = pl.ds((HEADS * source + h) * WIDTH, WIDTH)
            dk_out[:, at] = total[:, :WIDTH]
            dv_out[:, at] = total[:, WIDTH:]

    def send_outputs(h):
        away(od.at[:, peer_rows, head_lanes(h)], od_far.at[:, :, head_lanes(h)], o_send,
             o_recv, peer)

    for i, (src, dst) in enumerate(((k_hbm, k_in), (v_hbm, v_in))):
        near(src, dst, kv_in.at[i])
    for i, src in enumerate((q_hbm, g_hbm)):
        near(src.at[:, theirs], qg_in.at[i], qg_in_sem)
        near(src.at[:, mine], qg.at[i, token_rows], qg_own)

    zeros = jnp.zeros((BLOCK, 2 * WIDTH), jnp.float32)
    for t in range(CHIP_BLOCKS):
        parts[t, 0] = zeros
        parts[t, REACH + 1] = zeros
    base = chip * CHIP_BLOCKS
    begins, counts = [base + t for t in range(CHIP_BLOCKS)], [1] * CHIP_BLOCKS
    end = jnp.int32(0)
    for i in range(lengths.shape[0]):
        begin, end = end, end + lengths[i]
        for t in range(CHIP_BLOCKS):
            inside = (begin <= base + t) & (base + t < end)
            shown = jnp.where(fulls[i] > 0, end - begin, base + t - begin + 1)
            begins[t] = jnp.where(inside, begin, begins[t])
            counts[t] = jnp.where(inside, shown, counts[t])
    for t in range(CHIP_BLOCKS):
        first[t] = jnp.clip(begins[t] - base + OWN, t, t + OWN)
        seen[t] = counts[t]

    for kind, held in enumerate((k_in, v_in)):
        wait(held, kv_in.at[kind])
        for head in range(2 * HEADS):
            staged[head, kind] = held[:, :, pl.ds(head * WIDTH, WIDTH)]
    pl.semaphore_wait(barrier, 8)
    send_kv(0)
    wait(qg_in, qg_in_sem)
    send_queries(0)
    for h in range(HEADS):
        for kind in (0, 1):
            kv[h][kind, own_blocks] = staged[HEADS * core + h, kind]
    wait(qg_in, qg_own)
    for h in range(1, HEADS):
        wait(kv[h - 1].at[:, : WINDOW - 2], kv_send.at[h - 1])
        send_kv(h)
        send_queries(h)

    for h in range(HEADS):
        wait_inputs(h)
        tiles(h)
        send_partials(h)
        outputs(h)
        send_outputs(h)
    for i, dst in enumerate((o_hbm, dq_hbm)):
        near(od.at[i, token_rows], dst.at[:, mine], o_own)
    collect(0)
    wait(od_far, o_recv)
    for i, dst in enumerate((o_hbm, dq_hbm)):
        near(od_far.at[i], dst.at[:, theirs], o_far)
    collect(1)

    wait(kv[HEADS - 1].at[:, : WINDOW - 2], kv_send.at[HEADS - 1])
    for h in range(HEADS):
        wait(r[h], r_send.at[h])
    wait(qg_in, qg_send)
    wait(od_far, o_send)
    wait(od_far, o_own)
    wait(od_far, o_far)


def settle(*refs):
    refs, (loaded, stored) = refs[:-2], refs[-2:]
    count = len(refs) // 3
    steps = []
    for i in range(count):
        src, dst, held = refs[i], refs[count + i], refs[2 * count + i]
        pieces = PIECES if held.shape == refs[0].shape else 1
        size = held.shape[0] // pieces
        for piece in range(pieces):
            at = pl.ds(piece * size, size)
            load = pltpu.make_async_copy(src.at[at], held.at[at], loaded.at[i, piece])
            store = pltpu.make_async_copy(held.at[at], dst.at[at], stored.at[i, piece])
            load.start()
            steps.append((load, store))
    for load, store in steps:
        load.wait()
        store.start()
    for load, store in steps:
        store.wait()


def per_device(queries, key_vectors, value_matrix, out_grad, clip_lengths, clip_full):
    local, wide = queries.shape
    narrow = key_vectors.shape[1]
    half = wide // 2
    low = jnp.bfloat16
    whole = pl.BlockSpec(memory_space=pltpu.HBM)
    scalars = pl.BlockSpec(memory_space=pltpu.SMEM)
    near = pl.BlockSpec(memory_space=pltpu.VMEM)
    dma = pltpu.SemaphoreType.DMA

    def some(count, shape, dtype=low):
        return [pltpu.VMEM(shape, dtype)] * count

    shapes = [jax.ShapeDtypeStruct((local, n), low) for n in (wide, wide, narrow, narrow)]
    results = pl.pallas_call(
        kernel,
        out_shape=shapes,
        in_specs=[whole] * 4 + [scalars] * 2,
        out_specs=(whole, whole, near, near),
        scratch_shapes=[
            *some(2, (local // BLOCK, BLOCK, narrow)),
            pltpu.VMEM((2 * HEADS, 2, local // BLOCK, BLOCK, WIDTH), low),
            pltpu.VMEM((2, local, half), low),
            pltpu.VMEM((2, 2 * local, half), low),
            *some(HEADS, (2, WINDOW, BLOCK, WIDTH)),
            pltpu.VMEM((2, 2 * local, half), low),
            pltpu.VMEM((2, local, half), low),
            pltpu.VMEM((CHIP_BLOCKS, REACH + 2, BLOCK, 2 * WIDTH), jnp.float32),
            *some(2, (CHIP_BLOCKS, SPAN, half // HEADS // WIDTH * BLOCK)),
            *some(HEADS, (WINDOW * BLOCK, 2 * WIDTH)),
            *some(HEADS, (6, local, 2 * WIDTH)),
            pltpu.SMEM((CHIP_BLOCKS,), jnp.int32),
            pltpu.SMEM((CHIP_BLOCKS,), jnp.int32),
            dma((2,)), dma, dma, dma((HEADS,)), dma((HEADS,)), dma, dma((HEADS,)),
            dma((HEADS,)), dma((HEADS,)), dma, dma, dma, dma,
        ],
        compiler_params=pltpu.CompilerParams(
            collective_id=0, has_side_effects=True, vmem_limit_bytes=56 * 2**20
        ),
        cost_estimate=pl.CostEstimate(
            flops=12 * local * wide * SPAN,
            bytes_accessed=8 * local * (wide + narrow),
            transcendentals=local * wide // WIDTH * SPAN,
        ),
    )(
        queries,
        key_vectors.reshape(-1, BLOCK, narrow),
        value_matrix.reshape(-1, BLOCK, narrow),
        out_grad,
        clip_lengths,
        clip_full,
    )
    return pl.pallas_call(
        settle,
        out_shape=shapes,
        in_specs=[pl.BlockSpec(memory_space=pl.ANY)] * 4,
        out_specs=[whole] * 4,
        scratch_shapes=[
            *some(2, (local, wide)),
            *some(2, (local, narrow)),
            dma((4, PIECES)),
            dma((4, PIECES)),
        ],
        compiler_params=pltpu.CompilerParams(vmem_limit_bytes=56 * 2**20),
    )(*results)


def solution(mesh):
    sharded = P(("dp", "ctx"), None)
    return jax.shard_map(
        per_device,
        mesh=mesh,
        in_specs=(sharded, sharded, sharded, sharded, P("dp"), P("dp")),
        out_specs=(sharded, sharded, sharded, sharded),
        check_vma=False,
    )
```
